256 devices in a mesh: grp: 2 (over core), seq: 32 (over x, z), tp: 4 (over y).
Axes of the slice: x: 4, y: 4, z: 8, core: 2. Of those that a mesh axis runs over, the one named last changes fastest.
Arguments:
- neighbour_states: bfloat16 [64, 4, 128, 896], P('seq', 'tp'), may hold values from -64 to 64
- queries: bfloat16 [4096, 8192], P('seq', 'tp'), may hold values from -400 to 400
- out_grad: bfloat16 [4096, 8192], P('seq', 'tp'), may hold values from -6 to 6
- kv_weight: bfloat16 [2, 896, 8192], P('grp', None, 'tp'), may hold values from -0.1875 to 0.1875
- counts: int32 [64], replicated, may hold values from 0 to 4, as said below
- token_mask: int32 [64, 4, 128], replicated, may hold values from 0 to 1, as said below
Outputs:
- kv_grad: float32 [2, 896, 8192], P('grp', 'seq', 'tp')
The draws below stay inside these ranges and needn't reach their ends.
Inputs may be any that keep to these rules, and one draw needn't show every extreme that they name: `counts`: stretch 0 retrieves none, the last stretch 4, and every stretch c with c % 2 = 1 at least one. `token_mask`: in each neighbour block the ones form a prefix of 1 to 128 tokens.
All inputs are finite; a program needn't handle non-finite values.
Results may differ from the reference program's by a relative error of at most 0.0065.
The reference program's roundings to bfloat16 on the way (of `normed`, `probs_low`, `value_grads`, `score_grads` and `key_grads`) count: a program that leaves them out, or rounds other values in their place, can miss the bound.
Values may be sent and summed in bfloat16 or wider, within the bound.
A program may use at most 128 MiB of HBM per device.

```python
import math
import jax
import jax.numpy as jnp
from jax import lax

D = 8192
HD = 128
E = 896
SLOTS = 4
NLEN = 128
STRETCH = 64
CH_DEV = 2
STRETCHES = 64
TOKENS = 4096


def draw_neighbour_states(key, part):
    key = jax.random.fold_in(key, 5)
    key_base, key_rows, key_cols = jax.random.split(key, 3)
    shape = (STRETCHES, SLOTS, NLEN, E)
    row_scale = jnp.exp(jax.random.uniform(key_rows, (STRETCHES, SLOTS, NLEN, 1), jnp.float32, 0.0, math.log(10.0)))
    col_scale = jnp.exp(jax.random.uniform(key_cols, (E,), jnp.float32, math.log(0.3), math.log(3.0)))
    normals = jax.random.normal(key_base, shape, jnp.float32)
    return jnp.clip(normals * row_scale * col_scale, -64.0, 64.0).astype(jnp.bfloat16)


def draw_queries(key, part):
    key = jax.random.fold_in(key, 11)
    key_base = jax.random.fold_in(key, 0)
    normals = jnp.clip(jax.random.normal(key_base, (TOKENS, D), jnp.float32), -4.0, 4.0)
    return normals.astype(jnp.bfloat16)


def draw_token_mask(key, part):
    key = jax.random.fold_in(key, 17)
    lengths = jax.random.randint(key, (STRETCHES, SLOTS, 1), 1, NLEN + 1)
    positions = jnp.arange(NLEN, dtype=jnp.int32)[None, None, :]
    return (positions < lengths).astype(jnp.int32)


def draw_counts(key, part):
    key = jax.random.fold_in(key, 23)
    key_any, key_edge = jax.random.split(key)
    any_count = jax.random.randint(key_any, (STRETCHES,), 0, SLOTS + 1)
    edge_count = jax.random.randint(key_edge, (STRETCHES,), 1, SLOTS + 1)
    stretch_ids = jnp.arange(STRETCHES, dtype=jnp.int32)
    result = jnp.where(stretch_ids % CH_DEV == CH_DEV - 1, edge_count, any_count)
    result = jnp.where(stretch_ids == 0, 0, result)
    result = jnp.where(stretch_ids == STRETCHES - 1, SLOTS, result)
    return result.astype(jnp.int32)


def steps_of(own_key, extent, shards, low, largest):
    def one(dim, parts):
        steps = jax.random.uniform(jax.random.fold_in(jax.random.fold_in(own_key, 6), dim), (parts,), jnp.float32, low / len(shards), largest / len(shards))
        return jnp.repeat(jnp.exp(steps), extent[dim] // parts).reshape((-1,) + (1,) * (len(extent) - dim - 1))

    level = one(*shards[0])
    for cut in shards[1:]:
        level = level * one(*cut)
    return level


def normal_values(stream_key, shape, scale, bound, pieces=(), kind=jnp.bfloat16):
    factor_of = steps_of(stream_key, shape, pieces, -0.22, 0.18) if pieces else 1.0
    drawn = jax.random.normal(stream_key, shape, jnp.float32) * scale * factor_of
    return jnp.minimum(jnp.maximum(drawn, -bound), bound).astype(kind)


def setup_inputs(seed: int = 0) -> dict:
    key_of = jax.random.split(jax.random.key(seed), 7)
    return {
        "neighbour_states": draw_neighbour_states(jax.random.fold_in(key_of[6], 71), 0),
        "queries": draw_queries(jax.random.fold_in(key_of[6], 71), 0),
        "out_grad": normal_values(key_of[2], (TOKENS, D), 1.0, 6.0, ((0, 32), (1, 4))),
        "kv_weight": normal_values(key_of[3], (2, E, D), E ** -0.5, 0.1875, ((0, 2), (2, 4))),
        "counts": draw_counts(jax.random.fold_in(key_of[6], 71), 0),
        "token_mask": draw_token_mask(jax.random.fold_in(key_of[6], 71), 0),
    }


eps = 1e-06

def normalize(states):
    values_f = states.astype(jnp.float32)
    mean_sq = lax.optimization_barrier(jnp.mean(values_f * values_f, axis=-1, keepdims=True))
    return (values_f * lax.rsqrt(mean_sq + eps)).astype(jnp.bfloat16)

def key_valid(counts, token_mask):
    slot_ids = jnp.arange(SLOTS, dtype=jnp.int32)
    alive = (slot_ids[None, :] < counts[:, None])[:, :, None] & (token_mask > 0)
    return alive.reshape(counts.shape[0], SLOTS * NLEN)

def attend_back(query_tiles, key_tiles, value_tiles, out_tiles, live_keys):
    inv_root = HD ** (-0.5)
    scores = jnp.einsum('cqhd,ckhd->chqk', query_tiles.astype(jnp.float32), key_tiles.astype(jnp.float32)) * inv_root
    key_mask = live_keys[:, None, None, :]
    row_top = lax.optimization_barrier(jnp.max(jnp.where(key_mask, scores, -1000000000.0), axis=-1, keepdims=True))
    exponent = jnp.exp(jnp.where(key_mask, scores - row_top, -jnp.inf))
    row_total = jnp.maximum(lax.optimization_barrier(jnp.sum(exponent, axis=-1, keepdims=True)), 1.0)
    attn_probs = exponent / row_total
    probs_low = attn_probs.astype(jnp.bfloat16)
    value_grads = jnp.einsum('chqk,cqhd->ckhd', probs_low.astype(jnp.float32), out_tiles.astype(jnp.float32)).astype(jnp.bfloat16)
    prob_grads = jnp.einsum('cqhd,ckhd->chqk', out_tiles.astype(jnp.float32), value_tiles.astype(jnp.float32))
    row_delta = lax.optimization_barrier(jnp.sum(prob_grads * attn_probs, axis=-1, keepdims=True))
    score_grads = (attn_probs * (prob_grads - row_delta) * inv_root).astype(jnp.bfloat16)
    key_grads = jnp.einsum('chqk,cqhd->ckhd', score_grads.astype(jnp.float32), query_tiles.astype(jnp.float32)).astype(jnp.bfloat16)
    return (key_grads, value_grads)

def reference(neighbour_states, queries, out_grad, kv_weight, counts, token_mask):
    alive = key_valid(counts, token_mask)
    head_count = D // HD
    key_rows = SLOTS * NLEN

    def one_stretch(running, stretch_id):
        earlier = stretch_id - 1
        states = lax.dynamic_index_in_dim(neighbour_states, earlier, 0, keepdims=False).reshape(key_rows, E)
        normed = normalize(states)
        key_proj = jnp.dot(normed, kv_weight[0], preferred_element_type=jnp.float32).astype(jnp.bfloat16)
        value_proj = jnp.dot(normed, kv_weight[1], preferred_element_type=jnp.float32).astype(jnp.bfloat16)
        query_rows = lax.dynamic_slice_in_dim(queries, (stretch_id * STRETCH).astype(jnp.int32), STRETCH, 0)
        grad_rows = lax.dynamic_slice_in_dim(out_grad, (stretch_id * STRETCH).astype(jnp.int32), STRETCH, 0)
        live_keys = lax.dynamic_index_in_dim(alive, earlier, 0, keepdims=False)
        key_grads, value_grads = attend_back(query_rows.reshape(1, STRETCH, head_count, HD), key_proj.reshape(1, key_rows, head_count, HD), value_proj.reshape(1, key_rows, head_count, HD), grad_rows.reshape(1, STRETCH, head_count, HD), live_keys[None])
        dims = (((0,), (0,)), ((), ()))
        term_keys = lax.dot_general(normed, key_grads.reshape(key_rows, D), dims, preferred_element_type=jnp.float32)
        term_values = lax.dot_general(normed, value_grads.reshape(key_rows, D), dims, preferred_element_type=jnp.float32)
        return (running + jnp.stack([term_keys, term_values]), None)
    start_total = jnp.zeros((2, E, D), jnp.float32)
    running, _ = lax.scan(one_stretch, start_total, jnp.arange(1, STRETCHES, dtype=jnp.int32))
    return running
```

```python
import jax
import jax.numpy as jnp
from jax import lax
from jax.experimental import pallas as pl
from jax.experimental.pallas import tpu as pltpu
from jax.sharding import PartitionSpec as P

HD = 128
SLOTS = 4
NLEN = 128
STRETCH = 64
E = 896
ROWS = 28
PAD = 32
XS, ZS, TP = 4, 8, 4
SEQ = XS * ZS
COLS = 1024
PAIR = 2 * HD
PAIRS = COLS // PAIR
KEYS = SLOTS * NLEN
XC = 5
ZC = 3
EPS = 1e-06
CODED = False
WIRE = jnp.bfloat16 if CODED else jnp.float32
F32 = jnp.float32
BF16 = jnp.bfloat16
MESH = pl.DeviceIdType.MESH
FIRST, SECOND = slice(0, HD), slice(HD, 2 * HD)


def chains(size):
    far = size // 2
    found, start = [], 0
    for direction, half, steps in (
        (1, SECOND, far), (1, FIRST, far - 1), (-1, FIRST, far), (-1, SECOND, far - 1)
    ):
        found.append((direction, half, steps, start))
        start += steps
    return found


def encode(block):
    return block


def decode(message):
    return message


def kernel(
    counts, token_mask, states, queries, out_grad, weight, out,
    normed, weights, query_rows, grad_rows, chooser, turned, key_grads, value_grads, live,
    partial, sent_x, got_x, sent_z, got_z, mid_z, mid_x,
    sent_z2, got_z2, sent_x2, got_x2, final, swapped,
    local_sem, gs, gr, sx, rx, sz, rz, sz2, rz2, sx2, rx2,
):
    g = lax.axis_index("grp")
    s = lax.axis_index("seq")
    t = lax.axis_index("tp")
    x, z = lax.div(s, ZS), lax.rem(s, ZS)
    other = 1 - g
    t_up, t_down, t_far = lax.rem(t + 1, TP), lax.rem(t + TP - 1, TP), lax.rem(t + 2, TP)
    x_up = (g, lax.rem(x + 1, XS) * ZS + z, t)
    x_down = (g, lax.rem(x + XS - 1, XS) * ZS + z, t)
    z_up = (g, x * ZS + lax.rem(z + 1, ZS), t)
    z_down = (g, x * ZS + lax.rem(z + ZS - 1, ZS), t)
    s_up = (g, lax.rem(s + 1, SEQ), t)
    s_down = (g, lax.rem(s + SEQ - 1, SEQ), t)
    y_up, y_down, mate = (g, s, t_up), (g, s, t_down), (other, s, t)

    barrier = pltpu.get_barrier_semaphore()
    everyone = (mate, y_up, y_down, x_up, x_down, z_up, z_down, s_up, s_down)
    for device in everyone:
        pl.semaphore_signal(barrier, inc=1, device_id=device, device_id_type=MESH)

    own_cols = pl.ds(pl.multiple_of(g * COLS, COLS), COLS)
    mate_cols = pl.ds(pl.multiple_of(other * COLS, COLS), COLS)
    locals_ = [
        pltpu.make_async_copy(weight.at[0, :, own_cols], weights.at[g], local_sem.at[0]),
        pltpu.make_async_copy(
            queries.at[pl.ds(STRETCH, STRETCH), own_cols], query_rows.at[0], local_sem.at[1]
        ),
        pltpu.make_async_copy(
            out_grad.at[pl.ds(STRETCH, STRETCH), own_cols], grad_rows.at[0], local_sem.at[2]
        ),
    ]
    for copy in locals_:
        copy.start()

    for i in range(2):
        rows = states[i, 0].astype(F32)
        mean_sq = jnp.mean(rows * rows, axis=-1, keepdims=True)
        normed[i, t] = (rows * lax.rsqrt(mean_sq + EPS)).astype(BF16)

    pl.semaphore_wait(barrier, len(everyone))

    def remote(src, dst, index, device):
        return pltpu.make_async_remote_copy(
            src_ref=src, dst_ref=dst, send_sem=gs.at[index], recv_sem=gr.at[index],
            device_id=device, device_id_type=MESH,
        )

    low, high = pl.ds(0, NLEN // 2), pl.ds(NLEN // 2, NLEN // 2)
    mine = normed.at[g, t]
    below, above = normed.at[g, t_down], normed.at[g, t_up]
    far_low, far_high = normed.at[g, t_far, low], normed.at[g, t_far, high]
    to_up = remote(mine, mine, 0, y_up)
    to_down = remote(mine, mine, 1, y_down)
    to_up.start()
    to_down.start()
    weight_swap = remote(weight.at[0, :, mate_cols], weights.at[g], 8, mate)
    weight_swap.start()
    shift_q = remote(queries.at[pl.ds(0, STRETCH), own_cols], query_rows.at[1], 9, s_down)
    shift_g = remote(out_grad.at[pl.ds(0, STRETCH), own_cols], grad_rows.at[1], 10, s_down)
    shift_q.start()
    shift_g.start()

    def choose(b, carry):
        feature = lax.broadcasted_iota(jnp.int32, (PAD, E), 1)
        row = lax.broadcasted_iota(jnp.int32, (PAD, E), 0)
        hit = (feature - row == b * ROWS) & (row < ROWS)
        at = pl.ds(pl.multiple_of(b * PAD, PAD), PAD)
        chooser[at, :] = jnp.where(hit, 1.0, 0.0).astype(BF16)
        return carry

    lax.fori_loop(0, SEQ, choose, 0)

    for i in range(2):
        c = 2 * s + i
        count = jnp.where(c == 2 * SEQ - 1, 0, counts[c])
        lengths = jnp.sum(token_mask[c].astype(F32), axis=1, keepdims=True)
        token = lax.broadcasted_iota(jnp.int32, (NLEN, HD), 0).astype(F32)
        for j in range(SLOTS):
            bound = lengths[j : j + 1, :] * jnp.where(j < count, 1.0, 0.0)
            live[i, j * NLEN : (j + 1) * NLEN, :] = jnp.where(token < bound, 1.0, 0.0)

    def turn(slot):
        for i in range(2):
            at = pl.ds(pl.multiple_of(i * KEYS + slot * NLEN, NLEN), NLEN)
            turned[:, at] = lax.dot_general(
                chooser[...], normed[i, slot], (((1,), (1,)), ((), ())),
                preferred_element_type=F32,
            ).astype(BF16)

    turn_slot = lambda n, carry: (turn(lax.rem(t + n, TP)), carry)[1]

    remote(below, below, 0, y_down).wait_recv()
    up_half = remote(normed.at[g, t_down, low], normed.at[g, t_down, low], 2, y_up)
    up_half.start()
    mate_below = remote(below, below, 4, mate)
    mate_below.start()
    remote(above, above, 1, y_up).wait_recv()
    down_half = remote(normed.at[g, t_up, high], normed.at[g, t_up, high], 3, y_down)
    down_half.start()
    mate_above = remote(above, above, 5, mate)
    mate_above.start()
    turn(t)
    remote(far_low, far_low, 2, y_down).wait_recv()
    mate_far_low = remote(far_low, far_low, 6, mate)
    mate_far_low.start()
    remote(far_high, far_high, 3, y_up).wait_recv()
    mate_far_high = remote(far_high, far_high, 7, mate)
    mate_far_high.start()
    remote(normed.at[other, t_down], normed.at[other, t_down], 4, mate).wait_recv()
    remote(normed.at[other, t_up], normed.at[other, t_up], 5, mate).wait_recv()
    remote(normed.at[other, t_far, low], normed.at[other, t_far, low], 6, mate).wait_recv()
    remote(normed.at[other, t_far, high], normed.at[other, t_far, high], 7, mate).wait_recv()
    lax.fori_loop(1, TP, turn_slot, 0)
    for copy in locals_:
        copy.wait()
    remote(weight.at[0, :, mate_cols], weights.at[other], 8, mate).wait_recv()
    shift_q.wait_recv()
    shift_g.wait_recv()

    def message(sent, got, ssem, rsem, lead, n, device):
        return pltpu.make_async_remote_copy(
            src_ref=sent.at[(*lead, n)], dst_ref=got.at[(*lead, n)],
            send_sem=ssem.at[(*lead, n)], recv_sem=rsem.at[(*lead, n)],
            device_id=device, device_id_type=MESH,
        )

    def ring_step(size, me, up, down, step, own, lead, bufs):
        sent, got, ssem, rsem = bufs
        for direction, half, steps, start in chains(size):
            if steps < step:
                continue
            device = up if direction == 1 else down
            target = lax.rem(me + direction * (steps - step + 1) + size, size)
            block = own(target, half)
            n = start + step - 1
            if step > 1:
                message(sent, got, ssem, rsem, lead, n - 1, device).wait_recv()
                block = block + decode(got[(*lead, n - 1)])
            sent[(*lead, n)] = encode(block)
            message(sent, got, ssem, rsem, lead, n, device).start()

    def ring_last(size, me, up, down, own, lead, bufs, store):
        sent, got, ssem, rsem = bufs
        for half in (FIRST, SECOND):
            block = own(me, half)
            for direction, chain_half, steps, start in chains(size):
                if chain_half is half and steps:
                    n = start + steps - 1
                    device = up if direction == 1 else down
                    message(sent, got, ssem, rsem, lead, n, device).wait_recv()
                    block = block + decode(got[(*lead, n)])
            store(half, block)

    def ring_sent(size, up, down, lead, bufs):
        sent, got, ssem, rsem = bufs
        for direction, half, steps, start in chains(size):
            for n in range(start, start + steps):
                device = up if direction == 1 else down
                message(sent, got, ssem, rsem, lead, n, device).wait_send()

    bufs_x, bufs_z = (sent_x, got_x, sx, rx), (sent_z, got_z, sz, rz)
    bufs_z2, bufs_x2 = (sent_z2, got_z2, sz2, rz2), (sent_x2, got_x2, sx2, rx2)
    ring_x, ring_z = (XS, x, x_up, x_down), (ZS, z, z_up, z_down)

    def own_x(chunk):
        return lambda d, half: partial[chunk, d, :, :, half].reshape(ZS, PAD, HD)

    def own_z(chunk):
        return lambda d, half: partial[XC + chunk, :, d, :, half].reshape(XS, PAD, HD)

    def step_x(chunk, step):
        ring_step(*ring_x, step, own_x(chunk), (chunk,), bufs_x)

    def step_z(chunk, step):
        ring_step(*ring_z, step, own_z(chunk), (chunk,), bufs_z)

    root = HD**-0.5
    wide = (((1,), (1,)), ((), ()))

    def pair(p, carry):
        cols = pl.ds(pl.multiple_of(p * PAIR, PAIR), PAIR)

        def apart(rows):
            left = lax.broadcasted_iota(jnp.int32, rows.shape, 1) < HD
            rows = rows.astype(F32)
            return jnp.concatenate(
                [jnp.where(left, rows, 0.0), jnp.where(left, 0.0, rows)], 0
            ).astype(BF16)

        for i in range(2):
            tokens = normed[i].reshape(KEYS, E)
            keys = jnp.dot(tokens, weights[0, :, cols], preferred_element_type=F32).astype(BF16)
            values = jnp.dot(tokens, weights[1, :, cols], preferred_element_type=F32).astype(BF16)
            q = apart(query_rows[i, :, cols])
            og = apart(grad_rows[i, :, cols])
            alive = live[i] > 0.0
            scores = lax.dot_general(keys, q, wide, preferred_element_type=F32) * root
            top = jnp.max(jnp.where(alive, scores, -1000000000.0), axis=0, keepdims=True)
            weighed = jnp.where(alive, jnp.exp(scores - top), 0.0)
            total = jnp.maximum(jnp.sum(weighed, axis=0, keepdims=True), 1.0)
            probs = weighed / total
            rows_at = pl.ds(i * KEYS, KEYS)
            value_grads[rows_at, :] = jnp.dot(
                probs.astype(BF16), og, preferred_element_type=F32
            ).astype(BF16)
            prob_grads = lax.dot_general(values, og, wide, preferred_element_type=F32)
            delta = jnp.sum(prob_grads * probs, axis=0, keepdims=True)
            score_grads = (probs * (prob_grads - delta) * root).astype(BF16)
            key_grads[rows_at, :] = jnp.dot(
                score_grads, q, preferred_element_type=F32
            ).astype(BF16)

        value_chunk = jnp.where(p < ZC, XC + p, XC - 1)
        partial[p] = jnp.dot(
            turned[...], key_grads[...], preferred_element_type=F32
        ).reshape(XS, ZS, PAD, PAIR)
        step_x(p, 1)
        partial[value_chunk] = jnp.dot(
            turned[...], value_grads[...], preferred_element_type=F32
        ).reshape(XS, ZS, PAD, PAIR)

        @pl.when(p < ZC)
        def _():
            step_z(p, 1)

        @pl.when(p == ZC)
        def _():
            step_x(XC - 1, 1)

        return carry

    lax.fori_loop(0, PAIRS, pair, 0)

    def each(count, work):
        lax.fori_loop(0, count, lambda c, carry: (work(c), carry)[1], 0)

    def last_x(chunk):
        def store(half, block):
            mid_z[:, chunk, :, half] = block

        ring_last(*ring_x, own_x(chunk), (chunk,), bufs_x, store)

    def last_z(chunk):
        def store(half, block):
            mid_x[:, chunk, :, half] = block

        ring_last(*ring_z, own_z(chunk), (chunk,), bufs_z, store)

    own_z2 = lambda d, half: mid_z[d, :, :, half]
    own_x2 = lambda d, half: mid_x[d, :, :, half]
    step_z2 = lambda step: ring_step(*ring_z, step, own_z2, (), bufs_z2)
    step_x2 = lambda step: ring_step(*ring_x, step, own_x2, (), bufs_x2)

    each(ZC, lambda c: step_z(c, 2))
    each(XC, lambda c: step_x(c, 2))
    each(ZC, lambda c: step_z(c, 3))
    each(XC, last_x)
    step_z2(1)
    each(ZC, lambda c: step_z(c, 4))
    each(ZC, last_z)
    step_x2(1)
    step_z2(2)
    step_x2(2)
    step_z2(3)

    def store_x2(half, block):
        for c in range(ZC):
            final[1, :, c * PAIR + half.start : c * PAIR + half.stop] = block[c]

    ring_last(*ring_x, own_x2, (), bufs_x2, store_x2)
    step_z2(4)

    def store_z2(half, block):
        for c in range(XC):
            kind, p = (0, c) if c < PAIRS else (1, PAIRS - 1)
            final[kind, :, p * PAIR + half.start : p * PAIR + half.stop] = block[c]

    ring_last(*ring_z, own_z2, (), bufs_z2, store_z2)

    give = remote(final.at[other], swapped, 11, mate)
    give.start()
    out[0, :, own_cols] = final[g, :ROWS, :]
    give.wait_recv()
    out[0, :, mate_cols] = swapped[:ROWS, :]

    for copy in (
        to_up, to_down, up_half, down_half, mate_below, mate_above, mate_far_low, mate_far_high,
        weight_swap, shift_q, shift_g, give,
    ):
        copy.wait_send()
    each(XC, lambda c: ring_sent(XS, x_up, x_down, (c,), bufs_x))
    each(ZC, lambda c: ring_sent(ZS, z_up, z_down, (c,), bufs_z))
    ring_sent(ZS, z_up, z_down, (), bufs_z2)
    ring_sent(XS, x_up, x_down, (), bufs_x2)


def per_device(neighbour_states, queries, out_grad, kv_weight, counts, token_mask):
    x_msgs, z_msgs = 2 * XS - 2, 2 * ZS - 2
    vmem, dma = pltpu.VMEM, pltpu.SemaphoreType.DMA
    in_vmem = pl.BlockSpec(memory_space=pltpu.VMEM)
    anywhere = pl.BlockSpec(memory_space=pl.ANY)
    return pl.pallas_call(
        kernel,
        out_shape=jax.ShapeDtypeStruct((1, ROWS, 2 * COLS), F32),
        in_specs=[
            pl.BlockSpec(memory_space=pltpu.SMEM), in_vmem, in_vmem, anywhere, anywhere, anywhere,
        ],
        out_specs=in_vmem,
        scratch_shapes=[
            vmem((2, SLOTS, NLEN, E), BF16),
            vmem((2, E, COLS), BF16),
            vmem((2, STRETCH, COLS), BF16),
            vmem((2, STRETCH, COLS), BF16),
            vmem((SEQ * PAD, E), BF16),
            vmem((SEQ * PAD, 2 * KEYS), BF16),
            vmem((2 * KEYS, PAIR), BF16),
            vmem((2 * KEYS, PAIR), BF16),
            vmem((2, KEYS, HD), F32),
            vmem((XC + ZC, XS, ZS, PAD, PAIR), F32),
            vmem((XC, x_msgs, ZS, PAD, HD), WIRE),
            vmem((XC, x_msgs, ZS, PAD, HD), WIRE),
            vmem((ZC, z_msgs, XS, PAD, HD), WIRE),
            vmem((ZC, z_msgs, XS, PAD, HD), WIRE),
            vmem((ZS, XC, PAD, PAIR), F32),
            vmem((XS, ZC, PAD, PAIR), F32),
            vmem((z_msgs, XC, PAD, HD), WIRE),
            vmem((z_msgs, XC, PAD, HD), WIRE),
            vmem((x_msgs, ZC, PAD, HD), WIRE),
            vmem((x_msgs, ZC, PAD, HD), WIRE),
            vmem((2, PAD, COLS), F32),
            vmem((PAD, COLS), F32),
            dma((3,)),
            dma((12,)),
            dma((12,)),
            dma((XC, x_msgs)),
            dma((XC, x_msgs)),
            dma((ZC, z_msgs)),
            dma((ZC, z_msgs)),
            dma((z_msgs,)),
            dma((z_msgs,)),
            dma((x_msgs,)),
            dma((x_msgs,)),
        ],
        compiler_params=pltpu.CompilerParams(
            collective_id=0, has_side_effects=True, vmem_limit_bytes=56 * 1024 * 1024
        ),
        cost_estimate=pl.CostEstimate(
            flops=10_000_000_000, bytes_accessed=8_000_000, transcendentals=1_000_000
        ),
    )(counts, token_mask, neighbour_states, queries, out_grad, kv_weight)


def solution(mesh):
    return jax.shard_map(
        per_device,
        mesh=mesh,
        in_specs=(
            P("seq", "tp", None, None),
            P("seq", "tp"),
            P("seq", "tp"),
            P("grp", None, "tp"),
            P(),
            P(),
        ),
        out_specs=P("grp", "seq", "tp"),
        check_vma=False,
    )
```

```python
import jax
import jax.numpy as jnp
from jax import lax
from jax.experimental import pallas as pl
from jax.experimental.pallas import tpu as pltpu
from jax.sharding import PartitionSpec as P

HD = 128
SLOTS = 4
NLEN = 128
STRETCH = 64
E = 896
ROWS = 28
PAD = 32
XS, ZS, TP = 4, 8, 4
SEQ = XS * ZS
BAND = ZS * ROWS
COLS = 1024
PAIR = 2 * HD
PAIRS = COLS // PAIR
KEYS = SLOTS * NLEN
HALF = NLEN // 2
EPS = 1e-06
POWER = 9
SPAN = 2.0**13
F32 = jnp.float32
BF16 = jnp.bfloat16
MESH = pl.DeviceIdType.MESH
FIRST, SECOND, WHOLE = slice(0, HD), slice(HD, PAIR), slice(0, PAIR)


def with_children(edges):
    found = {}

    def visit(n):
        if n not in found:
            source, _, cols = edges[n]
            under = [m for m, (_, to, other) in enumerate(edges) if to == source and other == cols]
            found[n] = (*edges[n], under, 1 + max([visit(m)[4] for m in under], default=0))
        return found[n]

    return [visit(n) for n in range(len(edges))]


def around(size):
    far = size // 2
    edges = []
    for sign, cols, steps in (
        (-1, SECOND, far), (1, FIRST, far), (-1, FIRST, far - 1), (1, SECOND, far - 1)
    ):
        edges += [(sign * k, sign * (k - 1), cols) for k in range(steps, 0, -1)]
    return with_children(edges)


def direct(size):
    far = size // 2
    return with_children([(k, 0, WHOLE) for k in range(far, -far, -1) if k])


def strides(size):
    edges = []
    for sign, cols in ((1, FIRST), (-1, SECOND)):
        edges += [(4, 2, cols), (3, 2, cols), (-3, -2, cols)] if sign == 1 else [
            (-4, -2, cols), (-3, -2, cols), (3, 2, cols)
        ]
        edges += [(k, 0, cols) for k in (2, -2, 1, -1)]
    return with_children(edges)


X_FIRST = [(0, 0), (0, 1), (0, 2), (0, 3), (1, 3)]
Z_FIRST = [(1, 0), (1, 1), (1, 2)]
X_PLANS = [around(XS), around(XS), around(XS), direct(XS), direct(XS)]
Z_PLANS = [around(ZS), around(ZS), strides(ZS)]
THEN_Z = [([0, 1], strides(ZS)), ([2, 3, 4], direct(ZS))]
THEN_X = [([0, 1, 2], direct(XS))]
PHASES = (
    [(plan, 1, BAND + 16, BAND) for plan in X_PLANS]
    + [(plan, XS, PAD, ROWS) for plan in Z_PLANS]
    + [(plan, len(group), PAD, ROWS) for group, plan in THEN_Z]
    + [(plan, len(group), PAD, ROWS) for group, plan in THEN_X]
)


def encode(block, ref, valid):
    rows = ref.shape[1]
    largest = jnp.max(jnp.abs(block), axis=1, keepdims=True)
    scale = (jnp.maximum(largest, 1e-33) * 1.01).astype(BF16).astype(F32)
    unit = block * (SPAN / scale)
    square = unit * unit
    fourth = square * square
    powers = fourth * fourth * unit
    if block.shape[1] == rows:
        row = lax.broadcasted_iota(jnp.int32, block.shape, 1)
        ref[...] = jnp.where(row < valid, powers, scale).astype(BF16)
    else:
        ref[:, :valid, :] = powers.astype(BF16)
        wide = (block.shape[0], rows - valid, block.shape[2])
        ref[:, valid:, :] = jnp.broadcast_to(scale, wide).astype(BF16)


def decode(ref, valid):
    rows = ref.shape[1]
    if rows == PAD:
        powers = ref[...].astype(F32)
        row = lax.broadcasted_iota(jnp.int32, powers.shape, 1)
        scale = jnp.where(row < valid, powers[:, valid : valid + 1, :] * (1.0 / SPAN), 0.0)
    else:
        powers = ref[:, :valid, :].astype(F32)
        scale = ref[:, valid:, :].astype(F32)[:, :1, :] * (1.0 / SPAN)
    size = jnp.exp2(jnp.log2(jnp.maximum(jnp.abs(powers), 1e-37)) * (1.0 / POWER))
    return jnp.where(powers < 0.0, -scale, scale) * size


class Reduction:
    def __init__(self, phase, refs, me, device, own, store):
        self.plan, _, _, self.valid = phase
        self.sent, self.got, self.send_sem, self.recv_sem = refs
        self.me, self.device, self.own, self.store = me, device, own, store

    def copy(self, n):
        source, target, _, _, _ = self.plan[n]
        return pltpu.make_async_remote_copy(
            src_ref=self.sent.at[n], dst_ref=self.got.at[n],
            send_sem=self.send_sem.at[n], recv_sem=self.recv_sem.at[n],
            device_id=self.device(target - source), device_id_type=MESH,
        )

    def summed(self, offset, cols, under):
        block = self.own(self.me(-offset), cols)
        for n in under:
            self.copy(n).wait_recv()
            block = block + decode(self.got.at[n], self.valid)
        return block

    def step(self, step):
        for n, (source, _, cols, under, at) in enumerate(self.plan):
            if at == step:
                encode(self.summed(source, cols, under), self.sent.at[n], self.valid)
                self.copy(n).start()

    def last(self):
        for cols in sorted({edge[2].start for edge in self.plan}):
            under = [n for n, e in enumerate(self.plan) if e[1] == 0 and e[2].start == cols]
            cols = self.plan[under[0]][2]
            self.store(cols, self.summed(0, cols, under))

    def wait_sent(self):
        for n in range(len(self.plan)):
            self.copy(n).wait_send()


def kernel(
    counts, token_mask, states, queries, out_grad, weight, out,
    count_here, mask_here, states_here, normed, weights, query_rows, grad_rows, bias,
    projected, key_grads, value_grads, part_x, part_z, final, swapped, local_sem, gs, gr, *rest,
):
    g = lax.axis_index("grp")
    s = lax.axis_index("seq")
    t = lax.axis_index("tp")
    x, z = lax.div(s, ZS), lax.rem(s, ZS)
    other = 1 - g
    along_x = lambda by: (g, lax.rem(x + by + XS, XS) * ZS + z, t)
    along_z = lambda by: (g, x * ZS + lax.rem(z + by + ZS, ZS), t)
    s_up, s_down = (g, lax.rem(s + 1, SEQ), t), (g, lax.rem(s + SEQ - 1, SEQ), t)
    y_up, y_down = (g, s, lax.rem(t + 1, TP)), (g, s, lax.rem(t + TP - 1, TP))
    mate = (other, s, t)

    barrier = pltpu.get_barrier_semaphore()
    everyone = [mate, y_up, y_down, s_up, s_down]
    everyone += [along_x(by) for by in (1, -1, 2)]
    everyone += [along_z(by) for by in (1, -1, 2, -2, 3, -3, 4)]
    for device in everyone:
        pl.semaphore_signal(barrier, inc=1, device_id=device, device_id_type=MESH)

    own_cols = pl.ds(pl.multiple_of(g * COLS, COLS), COLS)
    mate_cols = pl.ds(pl.multiple_of(other * COLS, COLS), COLS)
    top_rows, bottom_rows = pl.ds(0, STRETCH), pl.ds(STRETCH, STRETCH)
    here = [
        pltpu.make_async_copy(source, target, local_sem.at[n])
        for n, (source, target) in enumerate((
            (states.at[:, 0], states_here),
            (token_mask.at[pl.ds(2 * s, 2)], mask_here),
            (counts, count_here),
            (weight.at[0, :, own_cols], weights.at[g]),
            (queries.at[bottom_rows, own_cols], query_rows.at[0]),
            (out_grad.at[bottom_rows, own_cols], grad_rows.at[0]),
        ))
    ]
    for copy in here:
        copy.start()

    def normalize(i):
        rows = states_here[i].astype(F32)
        mean_sq = jnp.mean(rows * rows, axis=-1, keepdims=True)
        normed[i, :NLEN, :] = (rows * lax.rsqrt(mean_sq + EPS)).astype(BF16)

    here[0].wait()
    normalize(g)
    pl.semaphore_wait(barrier, len(everyone))

    def remote(src, dst, index, device):
        return pltpu.make_async_remote_copy(
            src_ref=src, dst_ref=dst, send_sem=gs.at[index], recv_sem=gr.at[index],
            device_id=device, device_id_type=MESH,
        )

    def half(core, slot, high):
        return normed.at[core, pl.ds(slot * NLEN + high * HALF, HALF)]

    started = []

    def send(source, target, index, device):
        copy = remote(source, target, index, device)
        copy.start()
        started.append(copy)

    def arrived(piece, index):
        remote(piece, piece, index, mate).wait_recv()

    send(half(g, 0, 0), half(g, 3, 0), 0, y_up)
    send(half(g, 0, 1), half(g, 1, 1), 1, y_down)
    send(half(g, 0, 1), half(g, 3, 1), 2, y_up)
    send(half(g, 0, 0), half(g, 1, 0), 3, y_down)
    send(weight.at[0, :, mate_cols], weights.at[g], 12, mate)
    send(queries.at[top_rows, own_cols], query_rows.at[1], 13, s_down)
    send(out_grad.at[top_rows, own_cols], grad_rows.at[1], 14, s_down)

    normalize(other)

    def project(rows, stores, p):
        cols = pl.ds(pl.multiple_of(p * PAIR, PAIR), PAIR)
        for kind in range(2):
            result = jnp.dot(rows, weights[kind, :, cols], preferred_element_type=F32).astype(BF16)
            for n, (i, slot) in enumerate(stores):
                at = slice(slot * NLEN, (slot + 1) * NLEN)
                projected[kind, p, i, at, :] = result[n * NLEN : (n + 1) * NLEN, :]

    def project_slots(slots, p):
        stores = [(i, slot) for i in range(2) for slot in slots]
        rows = [normed[i, slot * NLEN : (slot + 1) * NLEN, :] for i, slot in stores]
        project(jnp.concatenate(rows, 0), stores, p)

    def each(start, stop, work):
        lax.fori_loop(start, stop, lambda c, carry: (work(c), carry)[1], 0)

    here[1].wait()
    here[2].wait()
    token = lax.broadcasted_iota(jnp.int32, (NLEN, HD), 0).astype(F32)
    for i in range(2):
        c = 2 * s + i
        count = jnp.where(c == 2 * SEQ - 1, 0, count_here[c])
        for n in range(SLOTS):
            slot = lax.rem(t + n, TP)
            length = jnp.sum(mask_here[i, pl.ds(slot, 1), :].astype(F32), axis=1, keepdims=True)
            bound = length * jnp.where(slot < count, 1.0, 0.0)
            bias[i, n * NLEN : (n + 1) * NLEN, :] = jnp.where(token < bound, 0.0, -1e30)

    arrived(half(g, 3, 0), 0)
    send(half(g, 3, 0), half(g, 2, 0), 4, y_up)
    arrived(half(g, 1, 1), 1)
    send(half(g, 1, 1), half(g, 2, 1), 5, y_down)
    send(half(g, 3, 0), half(g, 3, 0), 6, mate)
    send(half(g, 1, 1), half(g, 1, 1), 7, mate)
    for copy in here[3:]:
        copy.wait()
    arrived(weights.at[other], 12)
    each(0, 2, lambda p: project_slots([0], p))
    arrived(half(g, 3, 1), 2)
    send(half(g, 3, 1), half(g, 3, 1), 8, mate)
    arrived(half(g, 1, 0), 3)
    send(half(g, 1, 0), half(g, 1, 0), 9, mate)
    each(2, PAIRS, lambda p: project_slots([0], p))
    arrived(half(other, 3, 0), 6)
    arrived(half(other, 1, 1), 7)
    arrived(half(other, 3, 1), 8)
    arrived(half(other, 1, 0), 9)
    each(0, 1, lambda p: project_slots([1, 3], p))
    arrived(half(g, 2, 0), 4)
    send(half(g, 2, 0), half(g, 2, 0), 10, mate)
    arrived(half(g, 2, 1), 5)
    send(half(g, 2, 1), half(g, 2, 1), 11, mate)
    each(1, PAIRS, lambda p: project_slots([1, 3], p))
    arrived(query_rows.at[1], 13)
    arrived(grad_rows.at[1], 14)
    arrived(half(other, 2, 0), 10)
    arrived(half(other, 2, 1), 11)

    rest = list(rest)
    mids = [rest.pop(0) for _ in THEN_Z + THEN_X]
    refs = [tuple(rest[4 * n : 4 * n + 4]) for n in range(len(PHASES))]
    me_x = lambda by: lax.rem(x + by + XS, XS)
    me_z = lambda by: lax.rem(z + by + ZS, ZS)
    place = {}
    for n, (group, _) in enumerate(THEN_Z):
        place.update({X_FIRST[c]: (mids[n], k) for k, c in enumerate(group)})
    for n, (group, _) in enumerate(THEN_X):
        place.update({Z_FIRST[c]: (mids[len(THEN_Z) + n], k) for k, c in enumerate(group)})
    for ref in (part_z, *mids):
        ref[..., PAD - 8 :, :] = jnp.zeros((*ref.shape[:-2], 8, PAIR), F32)

    def first_x(n):
        mid, k = place[X_FIRST[n]]

        def store(cols, block):
            for b in range(ZS):
                mid[b, k, :ROWS, cols] = block[0, b * ROWS : (b + 1) * ROWS, :]

        own = lambda d, cols: part_x[n, d, :, cols].reshape(1, BAND, -1)
        return Reduction(PHASES[n], refs[n], me_x, along_x, own, store)

    def first_z(n):
        mid, k = place[Z_FIRST[n]]

        def store(cols, block):
            mid[:, k, :, cols] = block

        own = lambda d, cols: part_z[n, :, d, :, cols]
        m = len(X_FIRST) + n
        return Reduction(PHASES[m], refs[m], me_z, along_z, own, store)

    def then(m, mid, group, pieces, me, device):
        def store(cols, block):
            for k, c in enumerate(group):
                kind, p = pieces[c]
                final[kind, :, p * PAIR + cols.start : p * PAIR + cols.stop] = block[k]

        own = lambda d, cols: mid[d, :, :, cols]
        return Reduction(PHASES[m], refs[m], me, device, own, store)

    xs = [first_x(n) for n in range(len(X_FIRST))]
    zs = [first_z(n) for n in range(len(Z_FIRST))]
    m = len(xs) + len(zs)
    zz = [
        then(m + n, mids[n], group, X_FIRST, me_z, along_z)
        for n, (group, _) in enumerate(THEN_Z)
    ]
    m += len(zz)
    xx = [
        then(m + n, mids[len(zz) + n], group, Z_FIRST, me_x, along_x)
        for n, (group, _) in enumerate(THEN_X)
    ]

    root = HD**-0.5
    wide = (((1,), (1,)), ((), ()))

    def apart(rows):
        left = lax.broadcasted_iota(jnp.int32, rows.shape, 1) < HD
        rows = rows.astype(F32)
        return jnp.concatenate(
            [jnp.where(left, rows, 0.0), jnp.where(left, 0.0, rows)], 0
        ).astype(BF16)

    def attend(p):
        cols = pl.ds(pl.multiple_of(p * PAIR, PAIR), PAIR)
        for i in range(2):
            q, og = apart(query_rows[i, :, cols]), apart(grad_rows[i, :, cols])
            scores = lax.dot_general(projected[0, p, i], q, wide, preferred_element_type=F32)
            prob_grads = lax.dot_general(projected[1, p, i], og, wide, preferred_element_type=F32)
            scores = scores * root + bias[i]
            top = jnp.maximum(jnp.max(scores, axis=0, keepdims=True), -1e9)
            weighed = jnp.exp(scores - top)
            share = 1.0 / jnp.maximum(jnp.sum(weighed, axis=0, keepdims=True), 1.0)
            probs = weighed * share
            at = slice(i * KEYS, (i + 1) * KEYS)
            value_grads[at, :] = jnp.dot(
                probs.astype(BF16), og, preferred_element_type=F32
            ).astype(BF16)
            delta = jnp.sum(prob_grads * probs, axis=0, keepdims=True)
            score_grads = ((probs * root) * (prob_grads - delta)).astype(BF16)
            key_grads[at, :] = jnp.dot(score_grads, q, preferred_element_type=F32).astype(BF16)

    def gradient(grads):
        tokens = normed[...].reshape(2 * KEYS, E)
        return lax.dot_general(
            tokens, grads[...], (((0,), (0,)), ((), ())), preferred_element_type=F32
        )

    def after(p):
        if p == 0:
            zs[0].step(1)
        if p == 1:
            zs[1].step(1)
            xs[0].step(2)
            zs[0].step(2)
        if p == 2:
            zs[2].step(1)
            xs[1].step(2)
            xs[0].last()
            zs[0].step(3)
            zs[1].step(2)
        if p == 3:
            xs[4].step(1)
            xs[2].step(2)
            xs[1].last()
            zz[0].step(1)
            zs[2].step(2)
            zs[0].step(4)
            zs[1].step(3)

    def pair(p, carry):
        project_slots([2], p)
        attend(p)
        part_x[p] = gradient(key_grads).reshape(XS, BAND, PAIR)
        for n in range(PAIRS):
            pl.when(p == n)(lambda n=n: xs[n].step(1))

        @pl.when(p < PAIRS - 1)
        def _():
            result = gradient(value_grads)
            for b in range(SEQ):
                part_z[p, b // ZS, b % ZS, :ROWS, :] = result[b * ROWS : (b + 1) * ROWS, :]

        @pl.when(p == PAIRS - 1)
        def _():
            part_x[PAIRS] = gradient(value_grads).reshape(XS, BAND, PAIR)

        for n in range(PAIRS):
            pl.when(p == n)(lambda n=n: after(n))
        return carry

    lax.fori_loop(0, PAIRS, pair, 0)
    xs[2].last()
    zs[1].step(4)
    zs[0].last()
    zz[0].step(2)
    zs[2].last()
    xs[3].last()
    xs[4].last()
    zz[1].step(1)
    zs[1].last()
    xx[0].step(1)
    zz[0].last()
    xx[0].last()
    zz[1].last()

    give = remote(final.at[other], swapped, 15, mate)
    give.start()
    out[0, :, own_cols] = final[g, :ROWS, :]
    give.wait_recv()
    out[0, :, mate_cols] = swapped[:ROWS, :]

    for copy in (*started, give):
        copy.wait_send()
    for reduction in (*xs, *zs, *zz, *xx):
        reduction.wait_sent()


def per_device(neighbour_states, queries, out_grad, kv_weight, counts, token_mask):
    vmem, dma = pltpu.VMEM, pltpu.SemaphoreType.DMA
    anywhere = pl.BlockSpec(memory_space=pl.ANY)
    scratch = [
        pltpu.SMEM(counts.shape, jnp.int32),
        vmem((2, SLOTS, NLEN), jnp.int32),
        vmem((2, NLEN, E), BF16),
        vmem((2, KEYS, E), BF16),
        vmem((2, E, COLS), BF16),
        vmem((2, STRETCH, COLS), BF16),
        vmem((2, STRETCH, COLS), BF16),
        vmem((2, KEYS, HD), F32),
        vmem((2, PAIRS, 2, KEYS, PAIR), BF16),
        vmem((2 * KEYS, PAIR), BF16),
        vmem((2 * KEYS, PAIR), BF16),
        vmem((len(X_FIRST), XS, BAND, PAIR), F32),
        vmem((len(Z_FIRST), XS, ZS, PAD, PAIR), F32),
        vmem((2, PAD, COLS), F32),
        vmem((PAD, COLS), F32),
        dma((6,)),
        dma((16,)),
        dma((16,)),
    ]
    scratch += [vmem((ZS, len(group), PAD, PAIR), F32) for group, _ in THEN_Z]
    scratch += [vmem((XS, len(group), PAD, PAIR), F32) for group, _ in THEN_X]
    for plan, blocks, rows, _ in PHASES:
        width = plan[0][2].stop - plan[0][2].start
        scratch += [vmem((len(plan), blocks, rows, width), BF16)] * 2
        scratch += [dma((len(plan),))] * 2
    return pl.pallas_call(
        kernel,
        out_shape=jax.ShapeDtypeStruct((1, ROWS, 2 * COLS), F32),
        in_specs=[anywhere] * 6,
        out_specs=pl.BlockSpec(memory_space=pltpu.VMEM),
        scratch_shapes=scratch,
        compiler_params=pltpu.CompilerParams(
            collective_id=0, has_side_effects=True, vmem_limit_bytes=60 * 1024 * 1024
        ),
        cost_estimate=pl.CostEstimate(
            flops=10_000_000_000, bytes_accessed=8_000_000, transcendentals=1_000_000
        ),
    )(counts, token_mask, neighbour_states, queries, out_grad, kv_weight)


def solution(mesh):
    return jax.shard_map(
        per_device,
        mesh=mesh,
        in_specs=(
            P("seq", "tp", None, None),
            P("seq", "tp"),
            P("seq", "tp"),
            P("grp", None, "tp"),
            P(),
            P(),
        ),
        out_specs=P("grp", "seq", "tp"),
        check_vma=False,
    )
```

```python
import jax
import jax.numpy as jnp
from jax import lax
from jax.experimental import pallas as pl
from jax.experimental.pallas import tpu as pltpu
from jax.sharding import PartitionSpec as P

HD = 128
SLOTS = 4
NLEN = 128
STRETCH = 64
E = 896
ROWS = 28
PAD = 32
XS, ZS, TP = 4, 8, 4
SEQ = XS * ZS
BAND = ZS * ROWS
COLS = 1024
PAIR = 2 * HD
PAIRS = COLS // PAIR
KEYS = SLOTS * NLEN
HALF = NLEN // 2
EPS = 1e-06
POWER = 9
SPAN = 2.0**13
F32 = jnp.float32
BF16 = jnp.bfloat16
MESH = pl.DeviceIdType.MESH
FIRST, SECOND, WHOLE = slice(0, HD), slice(HD, PAIR), slice(0, PAIR)


def with_children(edges):
    found = {}

    def visit(n):
        if n not in found:
            source, _, cols = edges[n]
            under = [m for m, (_, to, other) in enumerate(edges) if to == source and other == cols]
            found[n] = (*edges[n], under, 1 + max([visit(m)[4] for m in under], default=0))
        return found[n]

    return [visit(n) for n in range(len(edges))]


def around(size):
    far = size // 2
    edges = []
    for sign, cols, steps in (
        (-1, SECOND, far), (1, FIRST, far), (-1, FIRST, far - 1), (1, SECOND, far - 1)
    ):
        edges += [(sign * k, sign * (k - 1), cols) for k in range(steps, 0, -1)]
    return with_children(edges)


def direct(size):
    far = size // 2
    return with_children([(k, 0, WHOLE) for k in range(far, -far, -1) if k])


def strides(size):
    edges = []
    for sign, cols in ((1, FIRST), (-1, SECOND)):
        edges += [(4, 2, cols), (3, 2, cols), (-3, -2, cols)] if sign == 1 else [
            (-4, -2, cols), (-3, -2, cols), (3, 2, cols)
        ]
        edges += [(k, 0, cols) for k in (2, -2, 1, -1)]
    return with_children(edges)


X_FIRST = [((1, 1), around(XS)), ((1, 2), around(XS)), ((0, 3), around(XS)), ((1, 3), around(XS))]
Z_FIRST = [((0, 0), around(ZS)), ((1, 0), around(ZS)), ((0, 1), around(ZS)), ((0, 2), around(ZS))]
THEN_Z = [([0], around(ZS)), ([1], strides(ZS)), ([2], strides(ZS)), ([3], direct(ZS))]
THEN_X = [([0, 1], around(XS)), ([2], direct(XS)), ([3], direct(XS))]
SCHEDULE = [
    [],
    [(4, 1), (5, 1)],
    [],
    [(6, 1), (0, 1)],
    [(4, 2), (5, 2)],
    [(7, 1), (1, 1), (6, 2), (0, 2)],
    [(4, 3)],
    [(5, 3), (2, 1), (3, 1), (7, 2), (1, 2), (6, 3), (4, 4), (0, 0), (8, 1), (5, 4), (2, 2), (7, 3), (6, 4), (3, 2), (8, 2), (4, 0), (5, 0), (12, 1), (7, 4), (1, 0), (9, 1), (2, 0), (8, 3), (10, 1), (6, 0), (12, 2), (13, 1), (3, 0), (11, 1), (7, 0), (14, 1), (8, 4), (9, 2), (12, 0), (10, 2), (13, 0), (14, 0), (8, 0), (11, 0), (9, 0), (10, 0)],
]
PHASES = (
    [(plan, 1, BAND + 16, BAND) for _, plan in X_FIRST]
    + [(plan, XS, PAD, ROWS) for _, plan in Z_FIRST]
    + [(plan, len(group), PAD, ROWS) for group, plan in THEN_Z]
    + [(plan, len(group), PAD, ROWS) for group, plan in THEN_X]
)


def encode(block, ref, valid):
    rows = ref.shape[1]
    largest = jnp.max(jnp.abs(block), axis=1, keepdims=True)
    scale = (jnp.maximum(largest, 1e-33) * 1.01).astype(BF16).astype(F32)
    unit = block * (SPAN / scale)
    square = unit * unit
    fourth = square * square
    powers = fourth * fourth * unit
    if block.shape[1] == rows:
        row = lax.broadcasted_iota(jnp.int32, block.shape, 1)
        ref[...] = jnp.where(row < valid, powers, scale).astype(BF16)
    else:
        ref[:, :valid, :] = powers.astype(BF16)
        wide = (block.shape[0], rows - valid, block.shape[2])
        ref[:, valid:, :] = jnp.broadcast_to(scale, wide).astype(BF16)


def decode(ref, valid):
    rows = ref.shape[1]
    if rows == PAD:
        powers = ref[...].astype(F32)
        row = lax.broadcasted_iota(jnp.int32, powers.shape, 1)
        scale = jnp.where(row < valid, powers[:, valid : valid + 1, :] * (1.0 / SPAN), 0.0)
    else:
        powers = ref[:, :valid, :].astype(F32)
        scale = ref[:, valid:, :].astype(F32)[:, :1, :] * (1.0 / SPAN)
    size = jnp.exp2(jnp.log2(jnp.maximum(jnp.abs(powers), 1e-37)) * (1.0 / POWER))
    return jnp.where(powers < 0.0, -scale, scale) * size


class Reduction:
    def __init__(self, phase, refs, me, device, own, store):
        self.plan, _, _, self.valid = phase
        self.sent, self.got, self.send_sem, self.recv_sem = refs
        self.me, self.device, self.own, self.store = me, device, own, store

    def copy(self, n):
        source, target, _, _, _ = self.plan[n]
        return pltpu.make_async_remote_copy(
            src_ref=self.sent.at[n], dst_ref=self.got.at[n],
            send_sem=self.send_sem.at[n], recv_sem=self.recv_sem.at[n],
            device_id=self.device(target - source), device_id_type=MESH,
        )

    def summed(self, offset, cols, under):
        block = self.own(self.me(-offset), cols)
        for n in under:
            self.copy(n).wait_recv()
            block = block + decode(self.got.at[n], self.valid)
        return block

    def step(self, step):
        for n, (source, _, cols, under, at) in enumerate(self.plan):
            if at == step:
                encode(self.summed(source, cols, under), self.sent.at[n], self.valid)
                self.copy(n).start()

    def last(self):
        for cols in sorted({edge[2].start for edge in self.plan}):
            under = [n for n, e in enumerate(self.plan) if e[1] == 0 and e[2].start == cols]
            cols = self.plan[under[0]][2]
            self.store(cols, self.summed(0, cols, under))

    def wait_sent(self):
        for n in range(len(self.plan)):
            self.copy(n).wait_send()


def kernel(
    counts, token_mask, states, queries, out_grad, weight, out,
    count_here, mask_here, states_here, normed, weights, query_rows, grad_rows, bias,
    projected, grads, part, part_z, final, swapped, local_sem, gs, gr, *rest,
):
    g = lax.axis_index("grp")
    s = lax.axis_index("seq")
    t = lax.axis_index("tp")
    x, z = lax.div(s, ZS), lax.rem(s, ZS)
    other = 1 - g
    along_x = lambda by: (g, lax.rem(x + by + XS, XS) * ZS + z, t)
    along_z = lambda by: (g, x * ZS + lax.rem(z + by + ZS, ZS), t)
    s_up, s_down = (g, lax.rem(s + 1, SEQ), t), (g, lax.rem(s + SEQ - 1, SEQ), t)
    y_up, y_down = (g, s, lax.rem(t + 1, TP)), (g, s, lax.rem(t + TP - 1, TP))
    mate = (other, s, t)

    barrier = pltpu.get_barrier_semaphore()
    everyone = [mate, y_up, y_down, s_up, s_down]
    everyone += [along_x(by) for by in (1, -1, 2)]
    everyone += [along_z(by) for by in (1, -1, 2, -2, 3, -3, 4)]
    for device in everyone:
        pl.semaphore_signal(barrier, inc=1, device_id=device, device_id_type=MESH)

    own_cols = pl.ds(pl.multiple_of(g * COLS, COLS), COLS)
    mate_cols = pl.ds(pl.multiple_of(other * COLS, COLS), COLS)
    top_rows, bottom_rows = pl.ds(0, STRETCH), pl.ds(STRETCH, STRETCH)
    here = [
        pltpu.make_async_copy(source, target, local_sem.at[n])
        for n, (source, target) in enumerate((
            (states.at[:, 0], states_here),
            (token_mask.at[pl.ds(2 * s, 2)], mask_here),
            (counts, count_here),
            (weight.at[0, :, own_cols], weights.at[g]),
            (queries.at[bottom_rows, own_cols], query_rows.at[0]),
            (out_grad.at[bottom_rows, own_cols], grad_rows.at[0]),
        ))
    ]
    for copy in here:
        copy.start()

    def normalize(i):
        rows = states_here[i].astype(F32)
        mean_sq = jnp.mean(rows * rows, axis=-1, keepdims=True)
        normed[i, :NLEN, :] = (rows * lax.rsqrt(mean_sq + EPS)).astype(BF16)

    here[0].wait()
    normalize(g)
    pl.semaphore_wait(barrier, len(everyone))

    def remote(src, dst, index, device):
        return pltpu.make_async_remote_copy(
            src_ref=src, dst_ref=dst, send_sem=gs.at[index], recv_sem=gr.at[index],
            device_id=device, device_id_type=MESH,
        )

    def half(core, slot, high):
        return normed.at[core, pl.ds(slot * NLEN + high * HALF, HALF)]

    started = []

    def send(source, target, index, device):
        copy = remote(source, target, index, device)
        copy.start()
        started.append(copy)

    def arrived(piece, index):
        remote(piece, piece, index, mate).wait_recv()

    send(half(g, 0, 0), half(g, 3, 0), 0, y_up)
    send(half(g, 0, 1), half(g, 1, 1), 1, y_down)
    send(half(g, 0, 1), half(g, 3, 1), 2, y_up)
    send(half(g, 0, 0), half(g, 1, 0), 3, y_down)
    send(weight.at[0, :, mate_cols], weights.at[g], 12, mate)
    send(queries.at[top_rows, own_cols], query_rows.at[1], 13, s_down)
    send(out_grad.at[top_rows, own_cols], grad_rows.at[1], 14, s_down)

    normalize(other)

    def project(rows, stores, p):
        cols = pl.ds(pl.multiple_of(p * PAIR, PAIR), PAIR)
        for kind in range(2):
            result = jnp.dot(rows, weights[kind, :, cols], preferred_element_type=F32).astype(BF16)
            for n, (i, slot) in enumerate(stores):
                at = slice(slot * NLEN, (slot + 1) * NLEN)
                projected[kind, p, i, at, :] = result[n * NLEN : (n + 1) * NLEN, :]

    def project_slots(slots, p):
        stores = [(i, slot) for i in range(2) for slot in slots]
        rows = [normed[i, slot * NLEN : (slot + 1) * NLEN, :] for i, slot in stores]
        project(jnp.concatenate(rows, 0), stores, p)

    def each(start, stop, work):
        lax.fori_loop(start, stop, lambda c, carry: (work(c), carry)[1], 0)

    here[1].wait()
    here[2].wait()
    token = lax.broadcasted_iota(jnp.int32, (NLEN, HD), 0).astype(F32)
    for i in range(2):
        c = 2 * s + i
        count = jnp.where(c == 2 * SEQ - 1, 0, count_here[c])
        for n in range(SLOTS):
            slot = lax.rem(t + n, TP)
            length = jnp.sum(mask_here[i, pl.ds(slot, 1), :].astype(F32), axis=1, keepdims=True)
            bound = length * jnp.where(slot < count, 1.0, 0.0)
            bias[i, n * NLEN : (n + 1) * NLEN, :] = jnp.where(token < bound, 0.0, -1e30)

    arrived(half(g, 3, 0), 0)
    send(half(g, 3, 0), half(g, 2, 0), 4, y_up)
    arrived(half(g, 1, 1), 1)
    send(half(g, 1, 1), half(g, 2, 1), 5, y_down)
    send(half(g, 3, 0), half(g, 3, 0), 6, mate)
    send(half(g, 1, 1), half(g, 1, 1), 7, mate)
    for copy in here[3:]:
        copy.wait()
    arrived(weights.at[other], 12)
    each(0, 2, lambda p: project_slots([0], p))
    arrived(half(g, 3, 1), 2)
    send(half(g, 3, 1), half(g, 3, 1), 8, mate)
    arrived(half(g, 1, 0), 3)
    send(half(g, 1, 0), half(g, 1, 0), 9, mate)
    each(2, PAIRS, lambda p: project_slots([0], p))
    arrived(half(other, 3, 0), 6)
    arrived(half(other, 1, 1), 7)
    arrived(half(other, 3, 1), 8)
    arrived(half(other, 1, 0), 9)
    each(0, 1, lambda p: project_slots([1, 3], p))
    arrived(half(g, 2, 0), 4)
    send(half(g, 2, 0), half(g, 2, 0), 10, mate)
    arrived(half(g, 2, 1), 5)
    send(half(g, 2, 1), half(g, 2, 1), 11, mate)
    each(1, PAIRS, lambda p: project_slots([1, 3], p))
    arrived(query_rows.at[1], 13)
    arrived(grad_rows.at[1], 14)
    arrived(half(other, 2, 0), 10)
    arrived(half(other, 2, 1), 11)

    rest = list(rest)
    mids = [rest.pop(0) for _ in THEN_Z + THEN_X]
    refs = [tuple(rest[4 * n : 4 * n + 4]) for n in range(len(PHASES))]
    me_x = lambda by: lax.rem(x + by + XS, XS)
    me_z = lambda by: lax.rem(z + by + ZS, ZS)
    place = {}
    for n, (group, _) in enumerate(THEN_Z):
        place.update({X_FIRST[c][0]: (mids[n], k) for k, c in enumerate(group)})
    for n, (group, _) in enumerate(THEN_X):
        place.update({Z_FIRST[c][0]: (mids[len(THEN_Z) + n], k) for k, c in enumerate(group)})
    for ref in (part_z, *mids):
        ref[..., PAD - 8 :, :] = jnp.zeros((*ref.shape[:-2], 8, PAIR), F32)

    def first_x(n):
        kind, p = X_FIRST[n][0]
        mid, k = place[kind, p]

        def store(cols, block):
            for b in range(ZS):
                mid[b, k, :ROWS, cols] = block[0, b * ROWS : (b + 1) * ROWS, :]

        def own(d, cols):
            at = slice(kind * PAIR + cols.start, kind * PAIR + cols.stop)
            return part[p, pl.ds(d, 1), :, at]

        return Reduction(PHASES[n], refs[n], me_x, along_x, own, store)

    def first_z(n):
        mid, k = place[Z_FIRST[n][0]]

        def store(cols, block):
            mid[:, k, :, cols] = block

        own = lambda d, cols: part_z[n, :, d, :, cols]
        m = len(X_FIRST) + n
        return Reduction(PHASES[m], refs[m], me_z, along_z, own, store)

    def then(m, mid, group, pieces, me, device):
        def store(cols, block):
            for k, c in enumerate(group):
                kind, p = pieces[c][0]
                final[kind, :, p * PAIR + cols.start : p * PAIR + cols.stop] = block[k]

        own = lambda d, cols: mid[d, :, :, cols]
        return Reduction(PHASES[m], refs[m], me, device, own, store)

    xs = [first_x(n) for n in range(len(X_FIRST))]
    zs = [first_z(n) for n in range(len(Z_FIRST))]
    m = len(xs) + len(zs)
    zz = [
        then(m + n, mids[n], group, X_FIRST, me_z, along_z)
        for n, (group, _) in enumerate(THEN_Z)
    ]
    m += len(zz)
    xx = [
        then(m + n, mids[len(zz) + n], group, Z_FIRST, me_x, along_x)
        for n, (group, _) in enumerate(THEN_X)
    ]

    root = HD**-0.5
    wide = (((1,), (1,)), ((), ()))

    def apart(rows):
        left = lax.broadcasted_iota(jnp.int32, rows.shape, 1) < HD
        rows = rows.astype(F32)
        return jnp.concatenate(
            [jnp.where(left, rows, 0.0), jnp.where(left, 0.0, rows)], 0
        ).astype(BF16)

    def attend(p):
        cols = pl.ds(pl.multiple_of(p * PAIR, PAIR), PAIR)
        both = range(2)
        q = [apart(query_rows[i, :, cols]) for i in both]
        og = [apart(grad_rows[i, :, cols]) for i in both]
        score = [
            lax.dot_general(projected[0, p, i], q[i], wide, preferred_element_type=F32) for i in both
        ]
        prob_grad = [
            lax.dot_general(projected[1, p, i], og[i], wide, preferred_element_type=F32) for i in both
        ]
        for i in both:
            scores = score[i] * root + bias[i]
            top = jnp.maximum(jnp.max(scores, axis=0, keepdims=True), -1e9)
            weighed = jnp.exp(scores - top)
            share = 1.0 / jnp.maximum(jnp.sum(weighed, axis=0, keepdims=True), 1.0)
            probs = weighed * share
            delta = jnp.sum(prob_grad[i] * probs, axis=0, keepdims=True)
            score_grads = ((probs * root) * (prob_grad[i] - delta)).astype(BF16)
            at = slice(i * KEYS, (i + 1) * KEYS)
            grads[at, PAIR:] = jnp.dot(
                probs.astype(BF16), og[i], preferred_element_type=F32
            ).astype(BF16)
            grads[at, :PAIR] = jnp.dot(score_grads, q[i], preferred_element_type=F32).astype(BF16)

    reductions = [*xs, *zs, *zz, *xx]

    def advance(actions):
        for n, step in actions:
            if step:
                reductions[n].step(step)
            else:
                reductions[n].last()

    def pad(n):
        kind, p = Z_FIRST[n][0]
        at = slice(kind * PAIR, (kind + 1) * PAIR)
        for b in range(SEQ):
            row = b % ZS * ROWS
            part_z[n, b // ZS, b % ZS, :ROWS, :] = part[p, b // ZS, row : row + ROWS, at]

    def after(p, actions):
        for n, (piece, _) in enumerate(Z_FIRST):
            if piece[1] == p:
                pad(n)
        advance(actions)

    def pair(p, carry):
        project_slots([2], p)
        attend(p)
        for n in range(PAIRS):
            if SCHEDULE[2 * n]:
                pl.when(p == n)(lambda n=n: advance(SCHEDULE[2 * n]))
        part[p] = lax.dot_general(
            normed[...].reshape(2 * KEYS, E), grads[...], (((0,), (0,)), ((), ())),
            preferred_element_type=F32,
        ).reshape(XS, BAND, 2 * PAIR)
        for n in range(PAIRS - 1):
            pl.when(p == n)(lambda n=n: after(n, SCHEDULE[2 * n + 1]))
        return carry

    lax.fori_loop(0, PAIRS, pair, 0)
    late = 6
    after(PAIRS - 1, SCHEDULE[-1][:-late])
    for copy in started:
        copy.wait_send()
    for reduction in (*xs, *zs):
        reduction.wait_sent()
    advance(SCHEDULE[-1][-late:])

    give = remote(final.at[other], swapped, 15, mate)
    give.start()
    out[0, :, own_cols] = final[g, :ROWS, :]
    give.wait_recv()
    out[0, :, mate_cols] = swapped[:ROWS, :]

    give.wait_send()
    for reduction in (*zz, *xx):
        reduction.wait_sent()


def per_device(neighbour_states, queries, out_grad, kv_weight, counts, token_mask):
    vmem, dma = pltpu.VMEM, pltpu.SemaphoreType.DMA
    in_hbm = pl.BlockSpec(memory_space=pltpu.HBM)
    scratch = [
        pltpu.SMEM(counts.shape, jnp.int32),
        vmem((2, SLOTS, NLEN), jnp.int32),
        vmem((2, NLEN, E), BF16),
        vmem((2, KEYS, E), BF16),
        vmem((2, E, COLS), BF16),
        vmem((2, STRETCH, COLS), BF16),
        vmem((2, STRETCH, COLS), BF16),
        vmem((2, KEYS, HD), F32),
        vmem((2, PAIRS, 2, KEYS, PAIR), BF16),
        vmem((2 * KEYS, 2 * PAIR), BF16),
        vmem((PAIRS, XS, BAND, 2 * PAIR), F32),
        vmem((len(Z_FIRST), XS, ZS, PAD, PAIR), F32),
        vmem((2, PAD, COLS), F32),
        vmem((PAD, COLS), F32),
        dma((6,)),
        dma((16,)),
        dma((16,)),
    ]
    scratch += [vmem((ZS, len(group), PAD, PAIR), F32) for group, _ in THEN_Z]
    scratch += [vmem((XS, len(group), PAD, PAIR), F32) for group, _ in THEN_X]
    for plan, blocks, rows, _ in PHASES:
        width = plan[0][2].stop - plan[0][2].start
        scratch += [vmem((len(plan), blocks, rows, width), BF16)] * 2
        scratch += [dma((len(plan),))] * 2
    return pl.pallas_call(
        kernel,
        out_shape=jax.ShapeDtypeStruct((1, ROWS, 2 * COLS), F32),
        in_specs=[in_hbm] * 6,
        out_specs=pl.BlockSpec(memory_space=pltpu.VMEM),
        scratch_shapes=scratch,
        compiler_params=pltpu.CompilerParams(
            collective_id=0, has_side_effects=True, vmem_limit_bytes=56 * 1024 * 1024
        ),
        cost_estimate=pl.CostEstimate(
            flops=10_000_000_000, bytes_accessed=8_000_000, transcendentals=1_000_000
        ),
    )(counts, token_mask, neighbour_states, queries, out_grad, kv_weight)


def solution(mesh):
    return jax.shard_map(
        per_device,
        mesh=mesh,
        in_specs=(
            P("seq", "tp", None, None),
            P("seq", "tp"),
            P("seq", "tp"),
            P("grp", None, "tp"),
            P(),
            P(),
        ),
        out_specs=P("grp", "seq", "tp"),
        check_vma=False,
    )
```

```python
import jax
import jax.numpy as jnp
from jax import lax
from jax.experimental import pallas as pl
from jax.experimental.pallas import tpu as pltpu
from jax.sharding import PartitionSpec as P

HD = 128
SLOTS = 4
NLEN = 128
STRETCH = 64
E = 896
ROWS = 28
PAD = 32
XS, ZS, TP = 4, 8, 4
SEQ = XS * ZS
BAND = ZS * ROWS
COLS = 1024
PAIR = 2 * HD
PAIRS = COLS // PAIR
KEYS = SLOTS * NLEN
HALF = NLEN // 2
EPS = 1e-06
POWER = 9
SPAN = 2.0**13
F32 = jnp.float32
BF16 = jnp.bfloat16
MESH = pl.DeviceIdType.MESH
FIRST, SECOND, WHOLE = slice(0, HD), slice(HD, PAIR), slice(0, PAIR)


def with_children(edges):
    found = {}

    def visit(n):
        if n not in found:
            source, _, cols = edges[n]
            under = [m for m, (_, to, other) in enumerate(edges) if to == source and other == cols]
            found[n] = (*edges[n], under, 1 + max([visit(m)[4] for m in under], default=0))
        return found[n]

    return [visit(n) for n in range(len(edges))]


def around(size):
    far = size // 2
    edges = []
    for sign, cols, steps in (
        (-1, SECOND, far), (1, FIRST, far), (-1, FIRST, far - 1), (1, SECOND, far - 1)
    ):
        edges += [(sign * k, sign * (k - 1), cols) for k in range(steps, 0, -1)]
    return with_children(edges)


def direct(size):
    far = size // 2
    return with_children([(k, 0, WHOLE) for k in range(far, -far, -1) if k])


def strides(size):
    edges = []
    for sign, cols in ((1, FIRST), (-1, SECOND)):
        edges += [(4, 2, cols), (3, 2, cols), (-3, -2, cols)] if sign == 1 else [
            (-4, -2, cols), (-3, -2, cols), (3, 2, cols)
        ]
        edges += [(k, 0, cols) for k in (2, -2, 1, -1)]
    return with_children(edges)


X_FIRST = [((0, 1), around(XS)), ((0, 2), around(XS)), ((0, 3), around(XS)), ((1, 3), around(XS))]
Z_FIRST = [((0, 0), around(ZS)), ((1, 0), around(ZS)), ((1, 1), around(ZS)), ((1, 2), around(ZS))]
THEN_Z = [([0], around(ZS)), ([1], strides(ZS)), ([2], strides(ZS)), ([3], direct(ZS))]
THEN_X = [([0], direct(XS)), ([1], direct(XS)), ([2], direct(XS)), ([3], direct(XS))]
SCHEDULE = [
    [],
    [(4, 1), (5, 1)],
    [],
    [(0, 1), (6, 1)],
    [(4, 2), (5, 2)],
    [(1, 1), (7, 1), (0, 2), (6, 2)],
    [(4, 3)],
    [(5, 3), (2, 1), (3, 1), (1, 2), (7, 2), (6, 3), (4, 4), (0, 0), (8, 1), (5, 4), (2, 2), (7, 3), (6, 4), (3, 2), (4, 0), (8, 2), (12, 1), (5, 0), (13, 1), (1, 0), (7, 4), (9, 1), (2, 0), (10, 1), (8, 3), (6, 0), (14, 1), (3, 0), (11, 1), (12, 0), (13, 0), (7, 0), (15, 1), (9, 2), (8, 4), (10, 2), (14, 0), (15, 0), (8, 0), (9, 0), (11, 0), (10, 0)],
]
PHASES = (
    [(plan, 1, BAND + 16, BAND) for _, plan in X_FIRST]
    + [(plan, XS, PAD, ROWS) for _, plan in Z_FIRST]
    + [(plan, len(group), PAD, ROWS) for group, plan in THEN_Z]
    + [(plan, len(group), PAD, ROWS) for group, plan in THEN_X]
)


def encode(block, ref, valid):
    rows = ref.shape[1]
    largest = jnp.max(jnp.abs(block), axis=1, keepdims=True)
    scale = (jnp.maximum(largest, 1e-33) * 1.01).astype(BF16).astype(F32)
    unit = block * (SPAN / scale)
    square = unit * unit
    fourth = square * square
    powers = fourth * fourth * unit
    if block.shape[1] == rows:
        row = lax.broadcasted_iota(jnp.int32, block.shape, 1)
        ref[...] = jnp.where(row < valid, powers, scale).astype(BF16)
    else:
        ref[:, :valid, :] = powers.astype(BF16)
        wide = (block.shape[0], rows - valid, block.shape[2])
        ref[:, valid:, :] = jnp.broadcast_to(scale, wide).astype(BF16)


def decode(ref, valid):
    rows = ref.shape[1]
    if rows == PAD:
        powers = ref[...].astype(F32)
        row = lax.broadcasted_iota(jnp.int32, powers.shape, 1)
        scale = jnp.where(row < valid, powers[:, valid : valid + 1, :] * (1.0 / SPAN), 0.0)
    else:
        powers = ref[:, :valid, :].astype(F32)
        scale = ref[:, valid:, :].astype(F32)[:, :1, :] * (1.0 / SPAN)
    size = jnp.exp2(jnp.log2(jnp.maximum(jnp.abs(powers), 1e-37)) * (1.0 / POWER))
    return jnp.where(powers < 0.0, -scale, scale) * size


class Reduction:
    def __init__(self, phase, refs, me, device, own, store):
        self.plan, self.valid = phase[0], phase[3]
        self.sent, self.got, self.send_sem, self.recv_sem = refs
        self.me, self.device, self.own, self.store = me, device, own, store

    def copy(self, n):
        source, target, _, _, _ = self.plan[n]
        return pltpu.make_async_remote_copy(
            src_ref=self.sent.at[n], dst_ref=self.got.at[n],
            send_sem=self.send_sem.at[n], recv_sem=self.recv_sem.at[n],
            device_id=self.device(target - source), device_id_type=MESH,
        )

    def summed(self, offset, cols, under):
        block = self.own(self.me(-offset), cols)
        for n in under:
            self.copy(n).wait_recv()
            block = block + decode(self.got.at[n], self.valid)
        return block

    def step(self, step):
        for n, (source, _, cols, under, at) in enumerate(self.plan):
            if at == step:
                encode(self.summed(source, cols, under), self.sent.at[n], self.valid)
                self.copy(n).start()

    def last(self):
        for cols in sorted({edge[2].start for edge in self.plan}):
            under = [n for n, e in enumerate(self.plan) if e[1] == 0 and e[2].start == cols]
            cols = self.plan[under[0]][2]
            self.store(cols, self.summed(0, cols, under))

    def wait_sent(self):
        for n in range(len(self.plan)):
            self.copy(n).wait_send()


class Ending(Reduction):
    def __init__(self, phase, refs, me, device, own, store, core, kind, mate):
        super().__init__(phase, refs, me, device, own, store)
        self.core, self.kind, self.mate = core, kind, mate
        self.widths = sorted({(edge[2].start, edge[2].stop) for edge in self.plan})

    def copy(self, n, source=None):
        source = self.core if source is None else source
        if n < len(self.plan):
            start, end = self.plan[n][:2]
            device = self.device(end - start)
            if end == 0:
                device = (self.kind, *device[1:])
        else:
            device = self.mate
        return pltpu.make_async_remote_copy(
            src_ref=self.sent.at[n], dst_ref=self.got.at[source, n],
            send_sem=self.send_sem.at[n], recv_sem=self.recv_sem.at[source, n],
            device_id=device, device_id_type=MESH,
        )

    def arrived(self, n, source):
        self.copy(n, source).wait_recv()
        return decode(self.got.at[source, n], self.valid)

    def summed(self, offset, cols, under):
        block = self.own(self.me(-offset), cols)
        for n in under:
            block = block + self.arrived(n, self.core)
        return block

    def step(self, step):
        if step == 1:

            @pl.when(self.core != self.kind)
            def _():
                for k, (start, stop) in enumerate(self.widths):
                    n = len(self.plan) + k
                    own = self.own(self.me(0), slice(start, stop))
                    encode(own, self.sent.at[n], self.valid)
                    self.copy(n).start()

        super().step(step)

    def last(self):
        @pl.when(self.core == self.kind)
        def _():
            for source in (self.kind, 1 - self.kind):
                for k, (start, stop) in enumerate(self.widths):
                    if source == self.kind:
                        block = self.own(self.me(0), slice(start, stop))
                    else:
                        block = self.arrived(len(self.plan) + k, source)
                    for n, (_, end, cols, _, _) in enumerate(self.plan):
                        if end == 0 and cols.start == start:
                            block = block + self.arrived(n, source)
                    self.store(source, slice(start, stop), block)

    def wait_sent(self):
        super().wait_sent()

        @pl.when(self.core != self.kind)
        def _():
            for k in range(len(self.widths)):
                self.copy(len(self.plan) + k).wait_send()


def kernel(
    counts, token_mask, states, queries, out_grad, weight, out,
    count_here, mask_here, states_here, normed, weights, query_rows, grad_rows, bias,
    projected, grads, part, part_z, local_sem, gs, gr, *rest,
):
    g = lax.axis_index("grp")
    s = lax.axis_index("seq")
    t = lax.axis_index("tp")
    x, z = lax.div(s, ZS), lax.rem(s, ZS)
    other = 1 - g
    along_x = lambda by: (g, lax.rem(x + by + XS, XS) * ZS + z, t)
    along_z = lambda by: (g, x * ZS + lax.rem(z + by + ZS, ZS), t)
    s_up, s_down = (g, lax.rem(s + 1, SEQ), t), (g, lax.rem(s + SEQ - 1, SEQ), t)
    y_up, y_down = (g, s, lax.rem(t + 1, TP)), (g, s, lax.rem(t + TP - 1, TP))
    mate = (other, s, t)

    barrier = pltpu.get_barrier_semaphore()
    everyone = [mate, y_up, y_down, s_up, s_down]
    everyone += [along_x(by) for by in (1, -1, 2)]
    everyone += [along_z(by) for by in (1, -1, 2, -2, 3, -3, 4)]
    everyone += [(other, *device[1:]) for device in everyone[5:]]
    for device in everyone:
        pl.semaphore_signal(barrier, inc=1, device_id=device, device_id_type=MESH)

    own_cols = pl.ds(pl.multiple_of(g * COLS, COLS), COLS)
    mate_cols = pl.ds(pl.multiple_of(other * COLS, COLS), COLS)
    top_rows, bottom_rows = pl.ds(0, STRETCH), pl.ds(STRETCH, STRETCH)
    here = [
        pltpu.make_async_copy(source, target, local_sem.at[n])
        for n, (source, target) in enumerate((
            (states.at[:, 0], states_here),
            (token_mask.at[pl.ds(2 * s, 2)], mask_here),
            (counts, count_here),
            (weight.at[0, :, own_cols], weights.at[g]),
            (queries.at[bottom_rows, own_cols], query_rows.at[0]),
            (out_grad.at[bottom_rows, own_cols], grad_rows.at[0]),
        ))
    ]
    for copy in here:
        copy.start()

    def normalize(i):
        rows = states_here[i].astype(F32)
        mean_sq = jnp.mean(rows * rows, axis=-1, keepdims=True)
        normed[i, :NLEN, :] = (rows * lax.rsqrt(mean_sq + EPS)).astype(BF16)

    here[0].wait()
    normalize(g)
    pl.semaphore_wait(barrier, len(everyone))

    def remote(src, dst, index, device):
        return pltpu.make_async_remote_copy(
            src_ref=src, dst_ref=dst, send_sem=gs.at[index], recv_sem=gr.at[index],
            device_id=device, device_id_type=MESH,
        )

    def half(core, slot, high):
        return normed.at[core, pl.ds(slot * NLEN + high * HALF, HALF)]

    started = []

    def send(source, target, index, device):
        copy = remote(source, target, index, device)
        copy.start()
        started.append(copy)

    def arrived(piece, index):
        remote(piece, piece, index, mate).wait_recv()

    send(half(g, 0, 0), half(g, 3, 0), 0, y_up)
    send(half(g, 0, 1), half(g, 1, 1), 1, y_down)
    send(half(g, 0, 1), half(g, 3, 1), 2, y_up)
    send(half(g, 0, 0), half(g, 1, 0), 3, y_down)
    send(weight.at[0, :, mate_cols], weights.at[g], 12, mate)
    send(queries.at[top_rows, own_cols], query_rows.at[1], 13, s_down)
    send(out_grad.at[top_rows, own_cols], grad_rows.at[1], 14, s_down)

    normalize(other)

    def project(rows, stores, p):
        cols = pl.ds(pl.multiple_of(p * PAIR, PAIR), PAIR)
        for kind in range(2):
            result = jnp.dot(rows, weights[kind, :, cols], preferred_element_type=F32).astype(BF16)
            for n, (i, slot) in enumerate(stores):
                at = slice(slot * NLEN, (slot + 1) * NLEN)
                projected[kind, p, i, at, :] = result[n * NLEN : (n + 1) * NLEN, :]

    def project_slots(slots, p):
        stores = [(i, slot) for i in range(2) for slot in slots]
        rows = [normed[i, slot * NLEN : (slot + 1) * NLEN, :] for i, slot in stores]
        project(jnp.concatenate(rows, 0), stores, p)

    def each(start, stop, work):
        lax.fori_loop(start, stop, lambda c, carry: (work(c), carry)[1], 0)

    here[1].wait()
    here[2].wait()
    token = lax.broadcasted_iota(jnp.int32, (NLEN, HD), 0).astype(F32)
    for i in range(2):
        c = 2 * s + i
        count = jnp.where(c == 2 * SEQ - 1, 0, count_here[c])
        for n in range(SLOTS):
            slot = lax.rem(t + n, TP)
            length = jnp.sum(mask_here[i, pl.ds(slot, 1), :].astype(F32), axis=1, keepdims=True)
            bound = length * jnp.where(slot < count, 1.0, 0.0)
            bias[i, n * NLEN : (n + 1) * NLEN, :] = jnp.where(token < bound, 0.0, -1e30)

    arrived(half(g, 3, 0), 0)
    send(half(g, 3, 0), half(g, 2, 0), 4, y_up)
    arrived(half(g, 1, 1), 1)
    send(half(g, 1, 1), half(g, 2, 1), 5, y_down)
    send(half(g, 3, 0), half(g, 3, 0), 6, mate)
    send(half(g, 1, 1), half(g, 1, 1), 7, mate)
    for copy in here[3:]:
        copy.wait()
    arrived(weights.at[other], 12)
    each(0, 2, lambda p: project_slots([0], p))
    arrived(half(g, 3, 1), 2)
    send(half(g, 3, 1), half(g, 3, 1), 8, mate)
    arrived(half(g, 1, 0), 3)
    send(half(g, 1, 0), half(g, 1, 0), 9, mate)
    each(2, PAIRS, lambda p: project_slots([0], p))
    arrived(half(other, 3, 0), 6)
    arrived(half(other, 1, 1), 7)
    arrived(half(other, 3, 1), 8)
    arrived(half(other, 1, 0), 9)
    each(0, 2, lambda p: project_slots([1, 3], p))
    arrived(half(g, 2, 0), 4)
    send(half(g, 2, 0), half(g, 2, 0), 10, mate)
    arrived(half(g, 2, 1), 5)
    send(half(g, 2, 1), half(g, 2, 1), 11, mate)
    each(2, PAIRS, lambda p: project_slots([1, 3], p))
    arrived(query_rows.at[1], 13)
    arrived(grad_rows.at[1], 14)
    arrived(half(other, 2, 0), 10)
    arrived(half(other, 2, 1), 11)

    rest = list(rest)
    mids = [rest.pop(0) for _ in THEN_Z + THEN_X]
    refs = [tuple(rest[4 * n : 4 * n + 4]) for n in range(len(PHASES))]
    me_x = lambda by: lax.rem(x + by + XS, XS)
    me_z = lambda by: lax.rem(z + by + ZS, ZS)
    place = {}
    for n, (group, _) in enumerate(THEN_Z):
        place.update({X_FIRST[c][0]: (mids[n], k) for k, c in enumerate(group)})
    for n, (group, _) in enumerate(THEN_X):
        place.update({Z_FIRST[c][0]: (mids[len(THEN_Z) + n], k) for k, c in enumerate(group)})
    for ref in (part_z, *mids):
        ref[..., PAD - 8 :, :] = jnp.zeros((*ref.shape[:-2], 8, PAIR), F32)

    def first_x(n):
        kind, p = X_FIRST[n][0]
        mid, k = place[kind, p]

        def store(cols, block):
            for b in range(ZS):
                mid[b, k, :ROWS, cols] = block[0, b * ROWS : (b + 1) * ROWS, :]

        def own(d, cols):
            at = slice(kind * PAIR + cols.start, kind * PAIR + cols.stop)
            return part[p, pl.ds(d, 1), :, at]

        return Reduction(PHASES[n], refs[n], me_x, along_x, own, store)

    def first_z(n):
        mid, k = place[Z_FIRST[n][0]]

        def store(cols, block):
            mid[:, k, :, cols] = block

        own = lambda d, cols: part_z[n, :, d, :, cols]
        m = len(X_FIRST) + n
        return Reduction(PHASES[m], refs[m], me_z, along_z, own, store)

    def then(m, mid, group, pieces, me, device):
        kind = pieces[group[0]][0][0]

        def store(source, cols, block):
            for k, c in enumerate(group):
                at = source * COLS + pieces[c][0][1] * PAIR
                out[0, :, at + cols.start : at + cols.stop] = block[k, :ROWS]

        own = lambda d, cols: mid[d, :, :, cols]
        return Ending(PHASES[m], refs[m], me, device, own, store, g, kind, mate)

    xs = [first_x(n) for n in range(len(X_FIRST))]
    zs = [first_z(n) for n in range(len(Z_FIRST))]
    m = len(xs) + len(zs)
    zz = [
        then(m + n, mids[n], group, X_FIRST, me_z, along_z)
        for n, (group, _) in enumerate(THEN_Z)
    ]
    m += len(zz)
    xx = [
        then(m + n, mids[len(zz) + n], group, Z_FIRST, me_x, along_x)
        for n, (group, _) in enumerate(THEN_X)
    ]

    root = HD**-0.5
    wide = (((1,), (1,)), ((), ()))

    def apart(rows):
        left = lax.broadcasted_iota(jnp.int32, rows.shape, 1) < HD
        rows = rows.astype(F32)
        return jnp.concatenate(
            [jnp.where(left, rows, 0.0), jnp.where(left, 0.0, rows)], 0
        ).astype(BF16)

    def attend(p):
        cols = pl.ds(pl.multiple_of(p * PAIR, PAIR), PAIR)
        both = range(2)
        q = [apart(query_rows[i, :, cols]) for i in both]
        og = [apart(grad_rows[i, :, cols]) for i in both]
        score = [
            lax.dot_general(projected[0, p, i], q[i], wide, preferred_element_type=F32) for i in both
        ]
        prob_grad = [
            lax.dot_general(projected[1, p, i], og[i], wide, preferred_element_type=F32) for i in both
        ]
        for i in both:
            scores = score[i] * root + bias[i]
            top = jnp.maximum(jnp.max(scores, axis=0, keepdims=True), -1e9)
            weighed = jnp.exp(scores - top)
            share = 1.0 / jnp.maximum(jnp.sum(weighed, axis=0, keepdims=True), 1.0)
            probs = weighed * share
            delta = jnp.sum(prob_grad[i] * probs, axis=0, keepdims=True)
            score_grads = ((probs * root) * (prob_grad[i] - delta)).astype(BF16)
            at = slice(i * KEYS, (i + 1) * KEYS)
            grads[at, PAIR:] = jnp.dot(
                probs.astype(BF16), og[i], preferred_element_type=F32
            ).astype(BF16)
            grads[at, :PAIR] = jnp.dot(score_grads, q[i], preferred_element_type=F32).astype(BF16)

    reductions = [*xs, *zs, *zz, *xx]

    def advance(actions):
        for n, step in actions:
            if step:
                reductions[n].step(step)
            else:
                reductions[n].last()

    def pad(n):
        kind, p = Z_FIRST[n][0]
        at = slice(kind * PAIR, (kind + 1) * PAIR)
        for b in range(SEQ):
            row = b % ZS * ROWS
            part_z[n, b // ZS, b % ZS, :ROWS, :] = part[p, b // ZS, row : row + ROWS, at]

    def after(p, actions):
        for n, (piece, _) in enumerate(Z_FIRST):
            if piece[1] == p:
                pad(n)
        advance(actions)

    def pair(p, carry):
        project_slots([2], p)
        attend(p)
        for n in range(PAIRS):
            if SCHEDULE[2 * n]:
                pl.when(p == n)(lambda n=n: advance(SCHEDULE[2 * n]))
        part[p] = lax.dot_general(
            normed[...].reshape(2 * KEYS, E), grads[...], (((0,), (0,)), ((), ())),
            preferred_element_type=F32,
        ).reshape(XS, BAND, 2 * PAIR)
        for n in range(PAIRS - 1):
            pl.when(p == n)(lambda n=n: after(n, SCHEDULE[2 * n + 1]))
        return carry

    lax.fori_loop(0, PAIRS, pair, 0)
    late = 6
    after(PAIRS - 1, SCHEDULE[-1][:-late])
    for copy in started:
        copy.wait_send()
    for reduction in (*xs, *zs):
        reduction.wait_sent()
    advance(SCHEDULE[-1][-late:])

    for reduction in (*zz, *xx):
        reduction.wait_sent()


def per_device(neighbour_states, queries, out_grad, kv_weight, counts, token_mask):
    vmem, dma = pltpu.VMEM, pltpu.SemaphoreType.DMA
    in_hbm = pl.BlockSpec(memory_space=pltpu.HBM)
    scratch = [
        pltpu.SMEM(counts.shape, jnp.int32),
        vmem((2, SLOTS, NLEN), jnp.int32),
        vmem((2, NLEN, E), BF16),
        vmem((2, KEYS, E), BF16),
        vmem((2, E, COLS), BF16),
        vmem((2, STRETCH, COLS), BF16),
        vmem((2, STRETCH, COLS), BF16),
        vmem((2, KEYS, HD), F32),
        vmem((2, PAIRS, 2, KEYS, PAIR), BF16),
        vmem((2 * KEYS, 2 * PAIR), BF16),
        vmem((PAIRS, XS, BAND, 2 * PAIR), F32),
        vmem((len(Z_FIRST), XS, ZS, PAD, PAIR), F32),
        dma((6,)),
        dma((15,)),
        dma((15,)),
    ]
    scratch += [vmem((ZS, len(group), PAD, PAIR), F32) for group, _ in THEN_Z]
    scratch += [vmem((XS, len(group), PAD, PAIR), F32) for group, _ in THEN_X]
    for n, (plan, blocks, rows, _) in enumerate(PHASES):
        width = plan[0][2].stop - plan[0][2].start
        if n < len(X_FIRST) + len(Z_FIRST):
            sends, receives = (len(plan),), (len(plan),)
        else:
            sends = (len(plan) + PAIR // width,)
            receives = (2, *sends)
        scratch += [vmem((*lead, blocks, rows, width), BF16) for lead in (sends, receives)]
        scratch += [dma(sends), dma(receives)]
    return pl.pallas_call(
        kernel,
        out_shape=jax.ShapeDtypeStruct((1, ROWS, 2 * COLS), F32),
        in_specs=[in_hbm] * 6,
        out_specs=pl.BlockSpec(memory_space=pltpu.VMEM),
        scratch_shapes=scratch,
        compiler_params=pltpu.CompilerParams(
            collective_id=0, has_side_effects=True, vmem_limit_bytes=56 * 1024 * 1024
        ),
        cost_estimate=pl.CostEstimate(
            flops=10_000_000_000, bytes_accessed=8_000_000, transcendentals=1_000_000
        ),
    )(counts, token_mask, neighbour_states, queries, out_grad, kv_weight)


def solution(mesh):
    return jax.shard_map(
        per_device,
        mesh=mesh,
        in_specs=(
            P("seq", "tp", None, None),
            P("seq", "tp"),
            P("seq", "tp"),
            P("grp", None, "tp"),
            P(),
            P(),
        ),
        out_specs=P("grp", "seq", "tp"),
        check_vma=False,
    )
```

```python
import jax
import jax.numpy as jnp
from jax import lax
from jax.experimental import pallas as pl
from jax.experimental.pallas import tpu as pltpu
from jax.sharding import PartitionSpec as P

HD = 128
SLOTS = 4
NLEN = 128
STRETCH = 64
E = 896
ROWS = 28
PAD = 32
XS, ZS, TP = 4, 8, 4
SEQ = XS * ZS
BAND = ZS * ROWS
COLS = 1024
PAIR = 2 * HD
PAIRS = COLS // PAIR
KEYS = SLOTS * NLEN
PIECES = 4
PIECE = NLEN // PIECES
EPS = 1e-06
POWER = 9
SPAN = 2.0**13
F32 = jnp.float32
BF16 = jnp.bfloat16
MESH = pl.DeviceIdType.MESH
FIRST, SECOND, WHOLE = slice(0, HD), slice(HD, PAIR), slice(0, PAIR)


def with_children(edges):
    found = {}

    def visit(n):
        if n not in found:
            source, _, cols = edges[n]
            under = [m for m, (_, to, other) in enumerate(edges) if to == source and other == cols]
            found[n] = (*edges[n], under, 1 + max([visit(m)[4] for m in under], default=0))
        return found[n]

    return [visit(n) for n in range(len(edges))]


def around(size):
    far = size // 2
    edges = []
    for sign, cols, steps in (
        (-1, SECOND, far), (1, FIRST, far), (-1, FIRST, far - 1), (1, SECOND, far - 1)
    ):
        edges += [(sign * k, sign * (k - 1), cols) for k in range(steps, 0, -1)]
    return with_children(edges)


def direct(size):
    far = size // 2
    return with_children([(k, 0, WHOLE) for k in range(far, -far, -1) if k])


def strides(size):
    edges = []
    for sign, cols in ((1, FIRST), (-1, SECOND)):
        edges += [(4, 2, cols), (3, 2, cols), (-3, -2, cols)] if sign == 1 else [
            (-4, -2, cols), (-3, -2, cols), (3, 2, cols)
        ]
        edges += [(k, 0, cols) for k in (2, -2, 1, -1)]
    return with_children(edges)


X_FIRST = [((0, 1), around(XS)), ((0, 2), around(XS)), ((0, 3), around(XS)), ((1, 3), around(XS))]
Z_FIRST = [((0, 0), around(ZS)), ((1, 0), around(ZS)), ((1, 1), around(ZS)), ((1, 2), around(ZS))]
THEN_Z = [([0], around(ZS)), ([1], strides(ZS)), ([2], strides(ZS)), ([3], direct(ZS))]
THEN_X = [([0], direct(XS)), ([1], direct(XS)), ([2], direct(XS)), ([3], direct(XS))]
SCHEDULE = [
    [],
    [(4, 1), (5, 1)],
    [],
    [(0, 1), (6, 1)],
    [(4, 2), (5, 2)],
    [(1, 1), (7, 1), (0, 2), (6, 2)],
    [(4, 3)],
    [(5, 3), (2, 1), (3, 1), (1, 2), (7, 2), (6, 3), (4, 4), (0, 0), (8, 1), (5, 4), (2, 2), (7, 3), (6, 4), (3, 2), (4, 0), (8, 2), (12, 1), (5, 0), (13, 1), (1, 0), (7, 4), (9, 1), (2, 0), (10, 1), (8, 3), (6, 0), (14, 1), (3, 0), (11, 1), (12, 0), (13, 0), (7, 0), (15, 1), (9, 2), (8, 4), (10, 2), (14, 0), (15, 0), (8, 0), (9, 0), (11, 0), (10, 0)],
]
PHASES = (
    [(plan, 1, BAND + 16, BAND) for _, plan in X_FIRST]
    + [(plan, XS, PAD, ROWS) for _, plan in Z_FIRST]
    + [(plan, len(group), PAD, ROWS) for group, plan in THEN_Z]
    + [(plan, len(group), PAD, ROWS) for group, plan in THEN_X]
)


def encode(block, ref, valid):
    rows = ref.shape[1]
    largest = jnp.max(jnp.abs(block), axis=1, keepdims=True)
    scale = (jnp.maximum(largest, 1e-33) * 1.01).astype(BF16).astype(F32)
    unit = block * (SPAN / scale)
    square = unit * unit
    fourth = square * square
    powers = fourth * fourth * unit
    if block.shape[1] == rows:
        row = lax.broadcasted_iota(jnp.int32, block.shape, 1)
        ref[...] = jnp.where(row < valid, powers, scale).astype(BF16)
    else:
        ref[:, :valid, :] = powers.astype(BF16)
        wide = (block.shape[0], rows - valid, block.shape[2])
        ref[:, valid:, :] = jnp.broadcast_to(scale, wide).astype(BF16)


def decode(ref, valid):
    rows = ref.shape[1]
    if rows == PAD:
        powers = ref[...].astype(F32)
        row = lax.broadcasted_iota(jnp.int32, powers.shape, 1)
        scale = jnp.where(row < valid, powers[:, valid : valid + 1, :] * (1.0 / SPAN), 0.0)
    else:
        powers = ref[:, :valid, :].astype(F32)
        scale = ref[:, valid:, :].astype(F32)[:, :1, :] * (1.0 / SPAN)
    size = jnp.exp2(jnp.log2(jnp.maximum(jnp.abs(powers), 1e-37)) * (1.0 / POWER))
    return jnp.where(powers < 0.0, -scale, scale) * size


class Reduction:
    def __init__(self, phase, refs, me, device, own, store):
        self.plan, self.valid = phase[0], phase[3]
        self.sent, self.got, self.send_sem, self.recv_sem = refs
        self.me, self.device, self.own, self.store = me, device, own, store

    def copy(self, n):
        source, target, _, _, _ = self.plan[n]
        return pltpu.make_async_remote_copy(
            src_ref=self.sent.at[n], dst_ref=self.got.at[n],
            send_sem=self.send_sem.at[n], recv_sem=self.recv_sem.at[n],
            device_id=self.device(target - source), device_id_type=MESH,
        )

    def summed(self, offset, cols, under):
        block = self.own(self.me(-offset), cols)
        for n in under:
            self.copy(n).wait_recv()
            block = block + decode(self.got.at[n], self.valid)
        return block

    def step(self, step):
        for n, (source, _, cols, under, at) in enumerate(self.plan):
            if at == step:
                encode(self.summed(source, cols, under), self.sent.at[n], self.valid)
                self.copy(n).start()

    def last(self):
        for cols in sorted({edge[2].start for edge in self.plan}):
            under = [n for n, e in enumerate(self.plan) if e[1] == 0 and e[2].start == cols]
            cols = self.plan[under[0]][2]
            self.store(cols, self.summed(0, cols, under))

    def wait_sent(self):
        for n in range(len(self.plan)):
            self.copy(n).wait_send()


class Ending(Reduction):
    def __init__(self, phase, refs, me, device, own, store, core, kind, mate):
        super().__init__(phase, refs, me, device, own, store)
        self.core, self.kind, self.mate = core, kind, mate
        self.widths = sorted({(edge[2].start, edge[2].stop) for edge in self.plan})

    def copy(self, n, source=None):
        source = self.core if source is None else source
        if n < len(self.plan):
            start, end = self.plan[n][:2]
            device = self.device(end - start)
            if end == 0:
                device = (self.kind, *device[1:])
        else:
            device = self.mate
        return pltpu.make_async_remote_copy(
            src_ref=self.sent.at[n], dst_ref=self.got.at[source, n],
            send_sem=self.send_sem.at[n], recv_sem=self.recv_sem.at[source, n],
            device_id=device, device_id_type=MESH,
        )

    def arrived(self, n, source):
        self.copy(n, source).wait_recv()
        return decode(self.got.at[source, n], self.valid)

    def summed(self, offset, cols, under):
        block = self.own(self.me(-offset), cols)
        for n in under:
            block = block + self.arrived(n, self.core)
        return block

    def step(self, step):
        if step == 1:

            @pl.when(self.core != self.kind)
            def _():
                for k, (start, stop) in enumerate(self.widths):
                    n = len(self.plan) + k
                    own = self.own(self.me(0), slice(start, stop))
                    encode(own, self.sent.at[n], self.valid)
                    self.copy(n).start()

        super().step(step)

    def last(self):
        @pl.when(self.core == self.kind)
        def _():
            for source in (self.kind, 1 - self.kind):
                for k, (start, stop) in enumerate(self.widths):
                    if source == self.kind:
                        block = self.own(self.me(0), slice(start, stop))
                    else:
                        block = self.arrived(len(self.plan) + k, source)
                    for n, (_, end, cols, _, _) in enumerate(self.plan):
                        if end == 0 and cols.start == start:
                            block = block + self.arrived(n, source)
                    self.store(source, slice(start, stop), block)

    def wait_sent(self):
        super().wait_sent()

        @pl.when(self.core != self.kind)
        def _():
            for k in range(len(self.widths)):
                self.copy(len(self.plan) + k).wait_send()


def kernel(
    counts, token_mask, states, queries, out_grad, weight, out,
    count_here, mask_here, states_here, normed, weights, query_rows, grad_rows, bias,
    projected, grads, part, part_z, local_sem, gs, gr, *rest,
):
    g = lax.axis_index("grp")
    s = lax.axis_index("seq")
    t = lax.axis_index("tp")
    x, z = lax.div(s, ZS), lax.rem(s, ZS)
    other = 1 - g
    along_x = lambda by: (g, lax.rem(x + by + XS, XS) * ZS + z, t)
    along_z = lambda by: (g, x * ZS + lax.rem(z + by + ZS, ZS), t)
    s_up, s_down = (g, lax.rem(s + 1, SEQ), t), (g, lax.rem(s + SEQ - 1, SEQ), t)
    y_up, y_down = (g, s, lax.rem(t + 1, TP)), (g, s, lax.rem(t + TP - 1, TP))
    mate = (other, s, t)

    barrier = pltpu.get_barrier_semaphore()
    everyone = [mate, y_up, y_down, s_up, s_down]
    everyone += [along_x(by) for by in (1, -1, 2)]
    everyone += [along_z(by) for by in (1, -1, 2, -2, 3, -3, 4)]
    everyone += [(other, *device[1:]) for device in everyone[5:]]
    for device in everyone:
        pl.semaphore_signal(barrier, inc=1, device_id=device, device_id_type=MESH)

    own_cols = pl.ds(pl.multiple_of(g * COLS, COLS), COLS)
    mate_cols = pl.ds(pl.multiple_of(other * COLS, COLS), COLS)
    top_rows, bottom_rows = pl.ds(0, STRETCH), pl.ds(STRETCH, STRETCH)
    here = [
        pltpu.make_async_copy(source, target, local_sem.at[n])
        for n, (source, target) in enumerate((
            (states.at[:, 0], states_here),
            (token_mask.at[pl.ds(2 * s, 2)], mask_here),
            (counts, count_here),
            (weight.at[0, :, own_cols], weights.at[g]),
            (queries.at[bottom_rows, own_cols], query_rows.at[0]),
            (out_grad.at[bottom_rows, own_cols], grad_rows.at[0]),
        ))
    ]
    for copy in here:
        copy.start()

    def normalize(i):
        rows = states_here[i].astype(F32)
        mean_sq = jnp.mean(rows * rows, axis=-1, keepdims=True)
        normed[i, :NLEN, :] = (rows * lax.rsqrt(mean_sq + EPS)).astype(BF16)

    here[0].wait()
    normalize(g)
    pl.semaphore_wait(barrier, len(everyone))

    def remote(src, dst, index, device):
        return pltpu.make_async_remote_copy(
            src_ref=src, dst_ref=dst, send_sem=gs.at[index], recv_sem=gr.at[index],
            device_id=device, device_id_type=MESH,
        )

    def piece(core, slot, n):
        return normed.at[core, pl.ds(slot * NLEN + n * PIECE, PIECE)]

    started = []

    def send(source, target, index, device):
        copy = remote(source, target, index, device)
        copy.start()
        started.append(copy)

    def arrived(piece, index):
        remote(piece, piece, index, mate).wait_recv()

    up_order = list(range(PIECES))
    down_order = up_order[PIECES // 2 :] + up_order[: PIECES // 2]
    lower, upper = up_order[: PIECES // 2], up_order[PIECES // 2 :]
    UP, DOWN, FAR, MATE = 0, PIECES, 2 * PIECES, 3 * PIECES
    for n, m in zip(up_order, down_order):
        send(piece(g, 0, n), piece(g, 3, n), UP + n, y_up)
        send(piece(g, 0, m), piece(g, 1, m), DOWN + m, y_down)
    send(weight.at[0, :, mate_cols], weights.at[g], 6 * PIECES, mate)
    send(queries.at[top_rows, own_cols], query_rows.at[1], 6 * PIECES + 1, s_down)
    send(out_grad.at[top_rows, own_cols], grad_rows.at[1], 6 * PIECES + 2, s_down)

    normalize(other)

    def project(rows, stores, p):
        cols = pl.ds(pl.multiple_of(p * PAIR, PAIR), PAIR)
        for kind in range(2):
            result = jnp.dot(rows, weights[kind, :, cols], preferred_element_type=F32).astype(BF16)
            for n, (i, slot) in enumerate(stores):
                at = slice(slot * NLEN, (slot + 1) * NLEN)
                projected[kind, p, i, at, :] = result[n * NLEN : (n + 1) * NLEN, :]

    def project_slots(slots, p):
        stores = [(i, slot) for i in range(2) for slot in slots]
        rows = [normed[i, slot * NLEN : (slot + 1) * NLEN, :] for i, slot in stores]
        project(jnp.concatenate(rows, 0), stores, p)

    def each(start, stop, work):
        lax.fori_loop(start, stop, lambda c, carry: (work(c), carry)[1], 0)

    here[1].wait()
    here[2].wait()
    token = lax.broadcasted_iota(jnp.int32, (NLEN, HD), 0).astype(F32)
    for i in range(2):
        c = 2 * s + i
        count = jnp.where(c == 2 * SEQ - 1, 0, count_here[c])
        for n in range(SLOTS):
            slot = lax.rem(t + n, TP)
            length = jnp.sum(mask_here[i, pl.ds(slot, 1), :].astype(F32), axis=1, keepdims=True)
            bound = length * jnp.where(slot < count, 1.0, 0.0)
            bias[i, n * NLEN : (n + 1) * NLEN, :] = jnp.where(token < bound, 0.0, -1e30)

    def pass_on(slot, n):
        index = MATE + (slot - 1) * PIECES + n
        send(piece(g, slot, n), piece(g, slot, n), index, mate)

    def passed(slots):
        for slot in slots:
            for n in range(PIECES):
                arrived(piece(other, slot, n), MATE + (slot - 1) * PIECES + n)

    for n, m in zip(lower, upper):
        arrived(piece(g, 3, n), UP + n)
        send(piece(g, 3, n), piece(g, 2, n), FAR + n, y_up)
        arrived(piece(g, 1, m), DOWN + m)
        send(piece(g, 1, m), piece(g, 2, m), FAR + m, y_down)
        pass_on(3, n)
        pass_on(1, m)
    for copy in here[3:]:
        copy.wait()
    arrived(weights.at[other], 6 * PIECES)
    each(0, 2, lambda p: project_slots([0], p))
    for n, m in zip(upper, lower):
        arrived(piece(g, 3, n), UP + n)
        pass_on(3, n)
        arrived(piece(g, 1, m), DOWN + m)
        pass_on(1, m)
    each(2, PAIRS, lambda p: project_slots([0], p))
    passed([3, 1])
    each(0, 1, lambda p: project_slots([1, 3], p))
    for n, m in zip(lower, upper):
        arrived(piece(g, 2, n), FAR + n)
        pass_on(2, n)
        arrived(piece(g, 2, m), FAR + m)
        pass_on(2, m)
    each(1, PAIRS, lambda p: project_slots([1, 3], p))
    arrived(query_rows.at[1], 6 * PIECES + 1)
    arrived(grad_rows.at[1], 6 * PIECES + 2)
    passed([2])

    rest = list(rest)
    mids = [rest.pop(0) for _ in THEN_Z + THEN_X]
    refs = [tuple(rest[4 * n : 4 * n + 4]) for n in range(len(PHASES))]
    me_x = lambda by: lax.rem(x + by + XS, XS)
    me_z = lambda by: lax.rem(z + by + ZS, ZS)
    place = {}
    for n, (group, _) in enumerate(THEN_Z):
        place.update({X_FIRST[c][0]: (mids[n], k) for k, c in enumerate(group)})
    for n, (group, _) in enumerate(THEN_X):
        place.update({Z_FIRST[c][0]: (mids[len(THEN_Z) + n], k) for k, c in enumerate(group)})
    for ref in (part_z, *mids):
        ref[..., PAD - 8 :, :] = jnp.zeros((*ref.shape[:-2], 8, PAIR), F32)

    def first_x(n):
        kind, p = X_FIRST[n][0]
        mid, k = place[kind, p]

        def store(cols, block):
            for b in range(ZS):
                mid[b, k, :ROWS, cols] = block[0, b * ROWS : (b + 1) * ROWS, :]

        def own(d, cols):
            at = slice(kind * PAIR + cols.start, kind * PAIR + cols.stop)
            return part[p, pl.ds(d, 1), :, at]

        return Reduction(PHASES[n], refs[n], me_x, along_x, own, store)

    def first_z(n):
        mid, k = place[Z_FIRST[n][0]]

        def store(cols, block):
            mid[:, k, :, cols] = block

        own = lambda d, cols: part_z[n, :, d, :, cols]
        m = len(X_FIRST) + n
        return Reduction(PHASES[m], refs[m], me_z, along_z, own, store)

    def then(m, mid, group, pieces, me, device):
        kind = pieces[group[0]][0][0]

        def store(source, cols, block):
            for k, c in enumerate(group):
                at = source * COLS + pieces[c][0][1] * PAIR
                out[0, :, at + cols.start : at + cols.stop] = block[k, :ROWS]

        own = lambda d, cols: mid[d, :, :, cols]
        return Ending(PHASES[m], refs[m], me, device, own, store, g, kind, mate)

    xs = [first_x(n) for n in range(len(X_FIRST))]
    zs = [first_z(n) for n in range(len(Z_FIRST))]
    m = len(xs) + len(zs)
    zz = [
        then(m + n, mids[n], group, X_FIRST, me_z, along_z)
        for n, (group, _) in enumerate(THEN_Z)
    ]
    m += len(zz)
    xx = [
        then(m + n, mids[len(zz) + n], group, Z_FIRST, me_x, along_x)
        for n, (group, _) in enumerate(THEN_X)
    ]

    root = HD**-0.5
    wide = (((1,), (1,)), ((), ()))

    def apart(rows):
        left = lax.broadcasted_iota(jnp.int32, rows.shape, 1) < HD
        rows = rows.astype(F32)
        return jnp.concatenate(
            [jnp.where(left, rows, 0.0), jnp.where(left, 0.0, rows)], 0
        ).astype(BF16)

    def attend(p):
        cols = pl.ds(pl.multiple_of(p * PAIR, PAIR), PAIR)
        both = range(2)
        q = [apart(query_rows[i, :, cols]) for i in both]
        og = [apart(grad_rows[i, :, cols]) for i in both]
        score = [
            lax.dot_general(projected[0, p, i], q[i], wide, preferred_element_type=F32) for i in both
        ]
        prob_grad = [
            lax.dot_general(projected[1, p, i], og[i], wide, preferred_element_type=F32) for i in both
        ]
        for i in both:
            scores = score[i] * root + bias[i]
            top = jnp.maximum(jnp.max(scores, axis=0, keepdims=True), -1e9)
            weighed = jnp.exp(scores - top)
            share = 1.0 / jnp.maximum(jnp.sum(weighed, axis=0, keepdims=True), 1.0)
            probs = weighed * share
            delta = jnp.sum(prob_grad[i] * probs, axis=0, keepdims=True)
            score_grads = ((probs * root) * (prob_grad[i] - delta)).astype(BF16)
            at = slice(i * KEYS, (i + 1) * KEYS)
            grads[at, PAIR:] = jnp.dot(
                probs.astype(BF16), og[i], preferred_element_type=F32
            ).astype(BF16)
            grads[at, :PAIR] = jnp.dot(score_grads, q[i], preferred_element_type=F32).astype(BF16)

    reductions = [*xs, *zs, *zz, *xx]

    def advance(actions):
        for n, step in actions:
            if step:
                reductions[n].step(step)
            else:
                reductions[n].last()

    def pad(n):
        kind, p = Z_FIRST[n][0]
        at = slice(kind * PAIR, (kind + 1) * PAIR)
        for b in range(SEQ):
            row = b % ZS * ROWS
            part_z[n, b // ZS, b % ZS, :ROWS, :] = part[p, b // ZS, row : row + ROWS, at]

    def after(p, actions):
        for n, (piece, _) in enumerate(Z_FIRST):
            if piece[1] == p:
                pad(n)
        advance(actions)

    def pair(p, carry):
        project_slots([2], p)
        attend(p)
        for n in range(PAIRS):
            if SCHEDULE[2 * n]:
                pl.when(p == n)(lambda n=n: advance(SCHEDULE[2 * n]))
        part[p] = lax.dot_general(
            normed[...].reshape(2 * KEYS, E), grads[...], (((0,), (0,)), ((), ())),
            preferred_element_type=F32,
        ).reshape(XS, BAND, 2 * PAIR)
        for n in range(PAIRS - 1):
            pl.when(p == n)(lambda n=n: after(n, SCHEDULE[2 * n + 1]))
        return carry

    lax.fori_loop(0, PAIRS, pair, 0)
    late = 6
    after(PAIRS - 1, SCHEDULE[-1][:-late])
    for copy in started:
        copy.wait_send()
    for reduction in (*xs, *zs):
        reduction.wait_sent()
    advance(SCHEDULE[-1][-late:])

    for reduction in (*zz, *xx):
        reduction.wait_sent()


def per_device(neighbour_states, queries, out_grad, kv_weight, counts, token_mask):
    vmem, dma = pltpu.VMEM, pltpu.SemaphoreType.DMA
    in_hbm = pl.BlockSpec(memory_space=pltpu.HBM)
    scratch = [
        pltpu.SMEM(counts.shape, jnp.int32),
        vmem((2, SLOTS, NLEN), jnp.int32),
        vmem((2, NLEN, E), BF16),
        vmem((2, KEYS, E), BF16),
        vmem((2, E, COLS), BF16),
        vmem((2, STRETCH, COLS), BF16),
        vmem((2, STRETCH, COLS), BF16),
        vmem((2, KEYS, HD), F32),
        vmem((2, PAIRS, 2, KEYS, PAIR), BF16),
        vmem((2 * KEYS, 2 * PAIR), BF16),
        vmem((PAIRS, XS, BAND, 2 * PAIR), F32),
        vmem((len(Z_FIRST), XS, ZS, PAD, PAIR), F32),
        dma((6,)),
        dma((6 * PIECES + 3,)),
        dma((6 * PIECES + 3,)),
    ]
    scratch += [vmem((ZS, len(group), PAD, PAIR), F32) for group, _ in THEN_Z]
    scratch += [vmem((XS, len(group), PAD, PAIR), F32) for group, _ in THEN_X]
    for n, (plan, blocks, rows, _) in enumerate(PHASES):
        width = plan[0][2].stop - plan[0][2].start
        if n < len(X_FIRST) + len(Z_FIRST):
            sends, receives = (len(plan),), (len(plan),)
        else:
            sends = (len(plan) + PAIR // width,)
            receives = (2, *sends)
        scratch += [vmem((*lead, blocks, rows, width), BF16) for lead in (sends, receives)]
        scratch += [dma(sends), dma(receives)]
    return pl.pallas_call(
        kernel,
        out_shape=jax.ShapeDtypeStruct((1, ROWS, 2 * COLS), F32),
        in_specs=[in_hbm] * 6,
        out_specs=pl.BlockSpec(memory_space=pltpu.VMEM),
        scratch_shapes=scratch,
        compiler_params=pltpu.CompilerParams(
            collective_id=0, has_side_effects=True, vmem_limit_bytes=56 * 1024 * 1024
        ),
        cost_estimate=pl.CostEstimate(
            flops=10_000_000_000, bytes_accessed=8_000_000, transcendentals=1_000_000
        ),
    )(counts, token_mask, neighbour_states, queries, out_grad, kv_weight)


def solution(mesh):
    return jax.shard_map(
        per_device,
        mesh=mesh,
        in_specs=(
            P("seq", "tp", None, None),
            P("seq", "tp"),
            P("seq", "tp"),
            P("grp", None, "tp"),
            P(),
            P(),
        ),
        out_specs=P("grp", "seq", "tp"),
        check_vma=False,
    )
```
